32 devices in a mesh: dp: 8 (over z, x), frame: 4 (over y, core).
Axes of the slice: x: 2, y: 2, z: 4, core: 2. Of those that a mesh axis runs over, the one named last changes fastest.
Arguments:
- enc_rows: bfloat16 [4096, 512], P(('dp', 'frame')), may hold values from -6 to 6
- dest: int32 [8, 4, 128], P(None, 'frame'), may hold values from 0 to 1023, as said below
- pred_rows: bfloat16 [1024, 512], P(('dp', 'frame')), may hold values from -6 to 6
- label_ids: int32 [8, 128], P('dp'), may hold values from 1 to 499
- block_off: int32 [64], P(('dp', 'frame')), may hold values from 0 to 64
- band_start: int32 [4096], P(('dp', 'frame')), may hold values from 0 to 61
- w_enc: bfloat16 [512, 512], replicated, may hold values from -0.25 to 0.25
- w_dec: bfloat16 [512, 512], replicated, may hold values from -0.25 to 0.25
- w_out: bfloat16 [512, 500], replicated
- bias_out: float32 [500], replicated, may hold values from -4 to 4
- grad_blank: float32 [4096, 3], P(('dp', 'frame')), may hold values from -6 to 6
- grad_label: float32 [4096, 3], P(('dp', 'frame')), may hold values from -6 to 6
Outputs:
- logprobs: float32 [4096, 6], P(('dp', 'frame'))
- grad_enc: bfloat16 [4096, 512], P(('dp', 'frame'))
- grad_pred: float32 [1024, 512], P(('dp', 'frame'))
- grad_w_out: float32 [512, 500], P(('dp', 'frame'))
The draws below stay inside these ranges and needn't reach their ends.
Inputs may be any that keep to these rules, and one draw needn't show every extreme that they name: For each frame shard f, dest[:, f, :] holds every value 0 to 1023 once; at most 32 rows of one loader shard go to one owner, exactly 32 for some pairs; the rows one loader shard sends one owner take consecutive owner rows, in increasing order of the sending shard.
All inputs are finite; a program needn't handle non-finite values.
Results may differ from the reference program's by a relative error of at most 0.01.
Values may be sent and summed in bfloat16 or wider, within the bound.
A program may use at most 64 MiB of HBM per device.

```python
import jax
import jax.numpy as jnp
from jax import lax

D = 512
DJ = 512
V = 500
PRUNE = 3
BLOCK = 64
ROWS_DEV = 128
OWNERS = 8
SHARDS = 4
CAP = 32
LABELS = 128
TOTAL_ROWS = 4096
LAB_ALL = 1024
BLOCKS_ALL = 64


def dest_column(key):
    key_pairs, key_perm, key_order = jax.random.split(key, 3)
    halves = OWNERS // 2
    first_half = jax.random.randint(key_pairs, (halves,), 0, CAP + 1).astype(jnp.int32)
    first_half = first_half.at[0].set(CAP)
    pattern = jnp.concatenate([first_half, CAP - first_half])
    pattern = pattern[jax.random.permutation(key_perm, OWNERS)]
    source_ids = jnp.arange(OWNERS, dtype=jnp.int32)
    pair_counts = pattern[(source_ids[None, :] - source_ids[:, None]) % OWNERS]
    owner_offsets = jnp.cumsum(pair_counts, axis=0) - pair_counts
    group_ends = jnp.cumsum(pair_counts, axis=1)
    group_starts = group_ends - pair_counts
    positions = jnp.arange(ROWS_DEV, dtype=jnp.int32)
    owner_of = jnp.sum((positions[None, :, None] >= group_ends[:, None, :]).astype(jnp.int32), axis=2)
    start_of = jnp.take_along_axis(group_starts, owner_of, axis=1)
    offset_of = jnp.take_along_axis(owner_offsets, owner_of, axis=1)
    ordered = owner_of * ROWS_DEV + offset_of + (positions[None, :] - start_of)
    scores = jax.random.randint(key_order, (OWNERS, ROWS_DEV), 0, 1 << 16).astype(jnp.int32) * ROWS_DEV + positions[None, :]
    shuffle = jnp.argsort(scores, axis=1)
    return jnp.take_along_axis(ordered, shuffle, axis=1)


def draw_dest(key, part):
    column_keys = jax.random.split(jax.random.fold_in(key, 11), SHARDS)
    columns = jax.vmap(dest_column)(column_keys)
    return columns.transpose(1, 0, 2).astype(jnp.int32)


def draw_w_out(key, part):
    key_main = jax.random.fold_in(jax.random.fold_in(key, 23), 0)
    weights = jax.random.normal(key_main, (DJ, V), jnp.float32) * DJ ** (-0.5)
    return weights.astype(jnp.bfloat16)


def plant(values, key, smallest, largest):
    shape = values.shape
    index_at = [jax.random.randint(jax.random.fold_in(key, axis), (), 0, shape[axis]) for axis in range(len(shape))]
    values = values.at[tuple(index_at)].set(smallest)
    longest = shape.index(max(shape))
    index_at[longest] = (index_at[longest] + 1) % shape[longest]
    return values.at[tuple(index_at)].set(largest)


def steps_of(own_key, dims, cuts, low, largest):
    gain, own = 1.0, jax.random.fold_in(own_key, 6)
    for axis_at, shards_of in cuts:
        draws = jnp.exp(jax.random.uniform(jax.random.fold_in(own, axis_at), (shards_of,), jnp.float32, low / len(cuts), largest / len(cuts)))
        gain = gain * jnp.repeat(draws, dims[axis_at] // shards_of).reshape([-1 if axis == axis_at else 1 for axis in range(len(dims))])
    return gain


def centred(rng, extent, deviation, bound, cuts=(), held_as=jnp.bfloat16):
    entries = deviation * jax.random.normal(rng, extent, jnp.float32)
    if cuts:
        entries = entries * steps_of(rng, extent, cuts, -0.22, 0.18)
    return jnp.clip(entries, -bound, bound).astype(held_as)


def setup_inputs(seed: int = 0) -> dict:
    arg_keys = jax.random.split(jax.random.key(seed), 13)
    enc_rows = centred(arg_keys[0], (TOTAL_ROWS, D), 1.0, 6.0, ((0, 32),))
    dest = draw_dest(jax.random.fold_in(arg_keys[12], 71), 0)
    pred_rows = centred(arg_keys[2], (LAB_ALL, D), 1.0, 6.0, ((0, 32),))
    label_ids = plant(jax.random.randint(arg_keys[3], (OWNERS, LABELS), 1, V), jax.random.fold_in(arg_keys[3], 1), 1, V - 1).astype(jnp.int32)
    block_off = plant(jax.random.randint(arg_keys[4], (BLOCKS_ALL,), 0, LABELS - BLOCK + 1), jax.random.fold_in(arg_keys[4], 1), 0, LABELS - BLOCK).astype(jnp.int32)
    band_start = plant(jax.random.randint(arg_keys[5], (TOTAL_ROWS,), 0, BLOCK - PRUNE + 1), jax.random.fold_in(arg_keys[5], 1), 0, BLOCK - PRUNE).astype(jnp.int32)
    w_enc = centred(arg_keys[6], (D, DJ), D ** -0.5, 0.25)
    w_dec = centred(arg_keys[7], (D, DJ), D ** -0.5, 0.25)
    w_out = draw_w_out(jax.random.fold_in(arg_keys[12], 71), 0)
    bias_out = centred(arg_keys[9], (V,), 1.0, 4.0, (), jnp.float32)
    grad_blank = centred(arg_keys[10], (TOTAL_ROWS, PRUNE), 1.0, 6.0, ((0, 32),), jnp.float32)
    grad_label = centred(arg_keys[11], (TOTAL_ROWS, PRUNE), 1.0, 6.0, ((0, 32),), jnp.float32)
    return {"enc_rows": enc_rows, "dest": dest, "pred_rows": pred_rows, "label_ids": label_ids, "block_off": block_off, "band_start": band_start, "w_enc": w_enc, "w_dec": w_dec, "w_out": w_out, "bias_out": bias_out, "grad_blank": grad_blank, "grad_label": grad_label}


def to_columns(array):
    return array.reshape(OWNERS, SHARDS, ROWS_DEV, -1).transpose(1, 0, 2, 3).reshape(SHARDS, OWNERS * ROWS_DEV, -1)


def from_columns(array):
    return array.reshape(SHARDS, OWNERS, ROWS_DEV, -1).transpose(1, 0, 2, 3).reshape(TOTAL_ROWS, -1)


def reference(enc_rows, dest, pred_rows, label_ids, block_off, band_start, w_enc, w_dec, w_out, bias_out, grad_blank, grad_label):
    dest_index = dest.transpose(1, 0, 2).reshape(SHARDS, OWNERS * ROWS_DEV).astype(jnp.int32)
    placed = jax.vmap(lambda values, where_to: jnp.zeros_like(values).at[where_to].set(values))(to_columns(enc_rows), dest_index)
    enc_owned = from_columns(placed)
    enc_joint = jnp.dot(enc_owned, w_enc, preferred_element_type=jnp.float32)
    dec_joint = jnp.dot(pred_rows, w_dec, preferred_element_type=jnp.float32).astype(jnp.bfloat16)
    flat_index = jnp.arange(TOTAL_ROWS, dtype=jnp.int32)
    owner_ids = flat_index // (SHARDS * ROWS_DEV)
    band_base = block_off[flat_index // BLOCK].astype(jnp.int32) + band_start
    label_flat = label_ids.reshape(-1)
    vocab_ids = jnp.arange(V, dtype=jnp.int32)
    enc_grad_j = jnp.zeros((TOTAL_ROWS, DJ), jnp.float32)
    dec_grad_j = jnp.zeros((LAB_ALL, DJ), jnp.float32)
    grad_w_out = jnp.zeros((DJ, V), jnp.float32)
    blank_cols = []
    label_cols = []
    for column in range(PRUNE):
        label_row = (owner_ids * LABELS + band_base + column).astype(jnp.int32)
        emitted = label_flat[label_row]
        hidden = jnp.tanh(enc_joint + dec_joint[label_row].astype(jnp.float32)).astype(jnp.bfloat16)
        logits = jnp.dot(hidden, w_out, preferred_element_type=jnp.float32) + bias_out
        logp = jax.nn.log_softmax(logits, axis=-1)
        blank_cols.append(logp[:, 0])
        label_cols.append(jnp.take_along_axis(logp, emitted[:, None], axis=1)[:, 0])
        cot_blank = grad_blank[:, column][:, None]
        cot_label = grad_label[:, column][:, None]
        dlogit = (cot_blank * (vocab_ids[None, :] == 0) + cot_label * (vocab_ids[None, :] == emitted[:, None])
                  - jnp.exp(logp) * (cot_blank + cot_label)).astype(jnp.bfloat16)
        grad_w_out = grad_w_out + lax.dot_general(hidden, dlogit, (((0,), (0,)), ((), ())), preferred_element_type=jnp.float32)
        back_hidden = lax.dot_general(dlogit, w_out, (((1,), (1,)), ((), ())), preferred_element_type=jnp.float32)
        hidden_f = hidden.astype(jnp.float32)
        dz_term = back_hidden * (1.0 - hidden_f * hidden_f)
        enc_grad_j = enc_grad_j + dz_term
        dec_grad_j = dec_grad_j.at[label_row].add(dz_term)
    logprobs = jnp.stack(blank_cols + label_cols, axis=1)
    owned_grad = lax.dot_general(enc_grad_j.astype(jnp.bfloat16), w_enc, (((1,), (1,)), ((), ())),
                                 preferred_element_type=jnp.float32).astype(jnp.bfloat16)
    taken = jax.vmap(lambda values, where_from: values[where_from])(to_columns(owned_grad), dest_index)
    grad_enc = from_columns(taken)
    grad_pred = jnp.dot(dec_grad_j, w_dec.astype(jnp.float32).T, precision=lax.Precision.HIGHEST)
    return logprobs, grad_enc, grad_pred, grad_w_out
```

```python
import functools

import jax
import jax.numpy as jnp
from jax import lax
from jax.experimental import pallas as pl
from jax.experimental.pallas import tpu as pltpu
from jax.sharding import PartitionSpec as P

BLOCK = 64
TILE_ROWS = 16
MASKED = -1e30
MESH = pl.DeviceIdType.MESH


def log2(size):
    assert size & (size - 1) == 0
    return size.bit_length() - 1


def joint_kernel(
    dims,
    enc_ref,
    dest_ref,
    pred_ref,
    label_ref,
    off_ref,
    band_ref,
    w_enc_ref,
    w_dec_ref,
    w_out_ref,
    bias_ref,
    blank_ref,
    cot_ref,
    logp_ref,
    grad_enc_ref,
    grad_pred_ref,
    grad_w_ref,
    outbound,
    arrived,
    outgoing,
    returned,
    pred_all,
    gw_send,
    gw_recv,
    gw2_send,
    gw2_recv,
    gp_send,
    gp_recv,
    dp_sem,
    frame_sem,
):
    owners, shards, cap, rows, kept, reduce_here = dims
    me = lax.axis_index("dp")
    part = lax.axis_index("frame")
    width = enc_ref.shape[1]
    joint = w_enc_ref.shape[1]
    vocab = w_out_ref.shape[0]
    lab_part = pred_ref.shape[0]
    labels = shards * lab_part
    slots = owners * cap
    f32, bf16 = jnp.float32, jnp.bfloat16

    def iota(shape, dim):
        return lax.broadcasted_iota(jnp.int32, shape, dim)

    def to_owner(step, src, dst, kind):
        peer = lax.rem(me + step, owners)
        return pltpu.make_async_remote_copy(
            src_ref=src(peer),
            dst_ref=dst(step),
            send_sem=dp_sem.at[kind, 0, step],
            recv_sem=dp_sem.at[kind, 1, step],
            device_id={"dp": peer},
            device_id_type=MESH,
        )

    def to_shard(step, src, dst, kind):
        peer = lax.rem(part + step, shards)
        return pltpu.make_async_remote_copy(
            src_ref=src(peer),
            dst_ref=dst(step),
            send_sem=frame_sem.at[kind, 0, step],
            recv_sem=frame_sem.at[kind, 1, step],
            device_id={"frame": peer},
            device_id_type=MESH,
        )

    def each(count, act):
        if count <= 8:
            for step in range(1, count):
                act(step)
        else:

            def body(step, carry):
                act(step)
                return carry

            lax.fori_loop(1, count, body, 0)

    barrier = pltpu.get_barrier_semaphore()

    def greet_owner(step):
        pl.semaphore_signal(
            barrier, inc=1, device_id={"dp": lax.rem(me + step, owners)}, device_id_type=MESH
        )

    def greet_shard(step):
        pl.semaphore_signal(
            barrier, inc=1, device_id={"frame": lax.rem(part + step, shards)}, device_id_type=MESH
        )

    each(owners, greet_owner)
    each(shards, greet_shard)

    shape = (slots, rows)
    slot_owner = lax.shift_right_logical(iota(shape, 0), log2(cap))
    slot_rank = iota(shape, 0) & (cap - 1)
    lane = iota(shape, 1)
    my_dest = dest_ref[pl.ds(me, 1), :]

    def count(source, sums):
        out_sum, in_sum = sums
        owner_of = lax.shift_right_logical(dest_ref[pl.ds(source, 1), :], log2(rows))
        before_me = (source < me).astype(f32)
        out_sum = out_sum + jnp.where(owner_of == slot_owner, before_me, 0.0)
        mine = jnp.where(owner_of == me, 1.0, 0.0)
        in_sum = in_sum + jnp.where(slot_owner > source, mine, 0.0)
        return out_sum, in_sum

    sums = (jnp.zeros(shape, f32), jnp.zeros(shape, f32))
    if owners <= 8:
        for source in range(owners):
            sums = count(source, sums)
    else:
        sums = lax.fori_loop(0, owners, count, sums)
    out_row = jnp.sum(sums[0], axis=1, keepdims=True).astype(jnp.int32) + slot_rank
    in_row = jnp.sum(sums[1], axis=1, keepdims=True).astype(jnp.int32) + slot_rank
    pick = (my_dest == slot_owner * rows + out_row) & (out_row < rows)
    pick = jnp.where(pick, 1.0, 0.0)
    place = jnp.where(lane == in_row, 1.0, 0.0)
    out_rows = jnp.dot(pick.astype(bf16), enc_ref[...], preferred_element_type=f32).astype(bf16)
    outbound[...] = out_rows.reshape(owners, cap, width)

    pl.semaphore_wait(barrier, owners - 1 + shards - 1)

    send_enc = functools.partial(
        to_owner, src=lambda peer: outbound.at[peer], dst=lambda step: arrived.at[me], kind=0
    )
    send_pred = functools.partial(
        to_shard, src=lambda peer: pred_ref, dst=lambda step: pred_all.at[part], kind=0
    )
    each(owners, lambda step: send_enc(step).start())
    each(shards, lambda step: send_pred(step).start())
    arrived[me] = outbound[me]
    pred_all[part] = pred_ref[...]

    half = iota((1, rows), 1) // BLOCK
    base_row = band_ref[...]
    for block in range(rows // BLOCK):
        base_row = base_row + jnp.where(half == block, off_ref[block], 0)
    cols = jnp.concatenate(
        [
            base_row.astype(f32),
            jnp.zeros((1, rows), f32),
            blank_ref[...],
            cot_ref[...],
        ],
        axis=0,
    ).T
    base_col = cols[:, 0:1].astype(jnp.int32)
    gather_hot = jnp.concatenate(
        [
            jnp.where(iota((rows, labels), 1) == base_col + k, 1.0, 0.0)
            for k in range(kept)
        ],
        axis=0,
    )
    scatter_hot = jnp.concatenate(
        [
            jnp.where(iota((labels, rows), 0) == base_row + k, 1.0, 0.0)
            for k in range(kept)
        ],
        axis=1,
    ).astype(bf16)
    emitted = jnp.sum(gather_hot * label_ref[...].astype(f32), axis=1, keepdims=True)
    emitted = emitted.astype(jnp.int32)
    place_t = place.T.astype(bf16)
    pick_t = pick.T.astype(bf16)
    place = place.astype(bf16)

    each(shards, lambda step: send_pred(step).wait())
    dec_joint = jnp.dot(
        pred_all[...].reshape(labels, width), w_dec_ref[...], preferred_element_type=f32
    ).astype(bf16)
    dec_rows = jnp.dot(gather_hot.astype(bf16), dec_joint, preferred_element_type=f32)

    each(owners, lambda step: send_enc(step).wait())
    enc_owned = jnp.dot(
        place_t, arrived[...].reshape(slots, width), preferred_element_type=f32
    ).astype(bf16)
    enc_joint = jnp.dot(enc_owned, w_enc_ref[...], preferred_element_type=f32)
    hidden = jnp.tanh(jnp.concatenate([enc_joint] * kept, axis=0) + dec_rows).astype(bf16)
    logits = (
        lax.dot_general(
            hidden, w_out_ref[...], (((1,), (1,)), ((), ())), preferred_element_type=f32
        )
        + bias_ref[...]
    )
    top = jnp.max(logits, axis=1, keepdims=True)
    shifted = logits - top
    powers = jnp.exp(shifted)
    total = jnp.sum(powers, axis=1, keepdims=True)
    log_total = jnp.log(total)
    word = iota((rows * kept, vocab), 1)
    is_label = word == emitted
    blank_logp = shifted[:, 0:1] - log_total
    label_logp = jnp.sum(jnp.where(is_label, shifted, 0.0), axis=1, keepdims=True) - log_total
    cot_blank = jnp.concatenate([cols[:, 2 + k : 3 + k] for k in range(kept)], axis=0)
    cot_label = jnp.concatenate([cols[:, 2 + kept + k : 3 + kept + k] for k in range(kept)], axis=0)
    scale = (cot_blank + cot_label) / total
    dlogit = (
        jnp.where(word == 0, cot_blank, 0.0) + jnp.where(is_label, cot_label, 0.0) - powers * scale
    ).astype(bf16)

    grad_w = lax.dot_general(
        hidden, dlogit, (((0,), (0,)), ((), ())), preferred_element_type=f32
    ).astype(bf16)
    if reduce_here:
        gw_send[...] = grad_w.reshape(gw_send.shape)
        send_gw = functools.partial(
            to_shard,
            src=lambda peer: gw_send.at[:, peer],
            dst=lambda step: gw_recv.at[step],
            kind=1,
        )
        each(shards, lambda step: send_gw(step).start())
    else:
        grad_w_ref[...] = grad_w.astype(f32)

    back = jnp.dot(dlogit, w_out_ref[...], preferred_element_type=f32)
    hidden_f = hidden.astype(f32)
    dz = back * (1.0 - hidden_f * hidden_f)
    enc_grad = dz[0:rows]
    for k in range(1, kept):
        enc_grad = enc_grad + dz[k * rows : (k + 1) * rows]
    owned_grad = lax.dot_general(
        enc_grad.astype(bf16), w_enc_ref[...], (((1,), (1,)), ((), ())), preferred_element_type=f32
    ).astype(bf16)
    outgoing[...] = (
        jnp.dot(place, owned_grad, preferred_element_type=f32)
        .astype(bf16)
        .reshape(owners, cap, width)
    )
    send_back = functools.partial(
        to_owner, src=lambda peer: outgoing.at[peer], dst=lambda step: returned.at[me], kind=1
    )
    each(owners, lambda step: send_back(step).start())
    returned[me] = outgoing[me]

    dec_grad = jnp.dot(scatter_hot, dz.astype(bf16), preferred_element_type=f32)
    gp_send[...] = (
        lax.dot_general(
            dec_grad.astype(bf16),
            w_dec_ref[...],
            (((1,), (1,)), ((), ())),
            preferred_element_type=f32,
        )
        .astype(bf16)
        .reshape(shards, lab_part, width)
    )
    send_gp = functools.partial(
        to_shard, src=lambda peer: gp_send.at[peer], dst=lambda step: gp_recv.at[step], kind=2
    )
    each(shards, lambda step: send_gp(step).start())

    if reduce_here:
        each(shards, lambda step: send_gw(step).wait())
        owner_sum = gw_send[:, part].astype(f32)
        for step in range(1, shards):
            owner_sum = owner_sum + gw_recv[step].astype(f32)
        gw2_send[...] = owner_sum.astype(bf16)
        send_gw2 = functools.partial(
            to_owner, src=lambda peer: gw2_send.at[peer], dst=lambda step: gw2_recv.at[step], kind=2
        )
        each(owners, lambda step: send_gw2(step).start())

    logp_cols = jnp.concatenate(
        [blank_logp[k * rows : (k + 1) * rows] for k in range(kept)]
        + [label_logp[k * rows : (k + 1) * rows] for k in range(kept)]
        + [jnp.zeros((rows, 8 - 2 * kept), f32)],
        axis=1,
    )
    logp_ref[...] = logp_cols.T[: 2 * kept]

    each(shards, lambda step: send_gp(step).wait())
    pred_sum = gp_send[part].astype(f32)
    for step in range(1, shards):
        pred_sum = pred_sum + gp_recv[step].astype(f32)
    grad_pred_ref[...] = pred_sum

    each(owners, lambda step: send_back(step).wait())
    grad_enc_ref[...] = jnp.dot(
        pick_t, returned[...].reshape(slots, width), preferred_element_type=f32
    ).astype(bf16)

    if reduce_here:
        each(owners, lambda step: send_gw2(step).wait())
        whole_sum = gw2_send[me].astype(f32)
        for step in range(1, owners):
            whole_sum = whole_sum + gw2_recv[step].astype(f32)
        grad_w_ref[...] = whole_sum


def shards_fn(
    enc_rows,
    dest,
    pred_rows,
    label_ids,
    block_off,
    band_start,
    w_enc,
    w_dec,
    w_out,
    bias_out,
    grad_blank,
    grad_label,
):
    owners = lax.axis_size("dp")
    shards = lax.axis_size("frame")
    rows, width = enc_rows.shape
    kept = grad_blank.shape[1]
    joint = w_enc.shape[1]
    vocab = w_out.shape[1]
    lab_part = pred_rows.shape[0]
    cap = max(TILE_ROWS, 2 * rows // owners)
    vocab_pad = -(-vocab // 128) * 128
    per_device = joint // (owners * shards)
    reduce_here = per_device % TILE_ROWS == 0
    grad_rows = per_device if reduce_here else joint
    slot_rows = per_device if reduce_here else TILE_ROWS
    slot_owners = owners if reduce_here else 1
    w_out_t = jnp.pad(w_out.T, ((0, vocab_pad - vocab), (0, 0)))
    bias = jnp.pad(bias_out, (0, vocab_pad - vocab), constant_values=MASKED)[None, :]
    bf16 = jnp.bfloat16
    vmem = pl.BlockSpec(memory_space=pltpu.VMEM)
    smem = pl.BlockSpec(memory_space=pltpu.SMEM)
    exchange = pltpu.VMEM((owners, cap, width), bf16)
    logp, grad_enc, grad_pred, grad_w = pl.pallas_call(
        functools.partial(joint_kernel, (owners, shards, cap, rows, kept, reduce_here)),
        out_shape=(
            jax.ShapeDtypeStruct((2 * kept, rows), jnp.float32),
            jax.ShapeDtypeStruct((rows, width), bf16),
            jax.ShapeDtypeStruct((lab_part, width), jnp.float32),
            jax.ShapeDtypeStruct((grad_rows, vocab_pad), jnp.float32),
        ),
        in_specs=[vmem] * 4 + [smem] + [vmem] * 7,
        out_specs=(vmem,) * 4,
        scratch_shapes=[
            exchange,
            exchange,
            exchange,
            exchange,
            pltpu.VMEM((shards, lab_part, width), bf16),
            pltpu.VMEM((slot_owners, shards, slot_rows, vocab_pad), bf16),
            pltpu.VMEM((shards, slot_owners, slot_rows, vocab_pad), bf16),
            pltpu.VMEM((slot_owners, slot_rows, vocab_pad), bf16),
            pltpu.VMEM((slot_owners, slot_rows, vocab_pad), bf16),
            pltpu.VMEM((shards, lab_part, width), bf16),
            pltpu.VMEM((shards, lab_part, width), bf16),
            pltpu.SemaphoreType.DMA((3, 2, owners)),
            pltpu.SemaphoreType.DMA((3, 2, shards)),
        ],
        compiler_params=pltpu.CompilerParams(
            collective_id=0, has_side_effects=True, vmem_limit_bytes=48 * 1024 * 1024
        ),
    )(
        enc_rows,
        dest[:, 0, :],
        pred_rows,
        label_ids,
        block_off,
        band_start[None, :],
        w_enc,
        w_dec,
        w_out_t,
        bias,
        grad_blank.T,
        grad_label.T,
    )
    if not reduce_here:
        grad_w = lax.psum_scatter(grad_w, ("dp", "frame"), scatter_dimension=0, tiled=True)
    return logp.T, grad_enc, grad_pred, grad_w[:, :vocab]


def solution(mesh):
    rows = P(("dp", "frame"), None)
    return jax.shard_map(
        shards_fn,
        mesh=mesh,
        in_specs=(
            rows,
            P(None, "frame", None),
            rows,
            P("dp", None),
            P(("dp", "frame")),
            P(("dp", "frame")),
            P(),
            P(),
            P(),
            P(),
            rows,
            rows,
        ),
        out_specs=(rows, rows, rows, rows),
        check_vma=False,
    )
```

```python
import functools

import jax
import jax.numpy as jnp
from jax import lax
from jax.experimental import pallas as pl
from jax.experimental.pallas import tpu as pltpu
from jax.sharding import PartitionSpec as P

BLOCK = 64
TILE_ROWS = 16
VMEM_BYTES = 64 * 1024 * 1024
MESH = pl.DeviceIdType.MESH


def log2(size):
    assert size & (size - 1) == 0
    return size.bit_length() - 1


def joint_kernel(
    dims,
    enc_hbm,
    dest_hbm,
    pred_ref,
    label_hbm,
    off_hbm,
    band_hbm,
    w_enc_hbm,
    w_dec_hbm,
    w_out_hbm,
    bias_hbm,
    blank_hbm,
    cot_hbm,
    logp_hbm,
    grad_enc_hbm,
    grad_pred_hbm,
    grad_w_hbm,
    outbound,
    arrived,
    outgoing,
    returned,
    pred_all,
    gw_send,
    gw_recv,
    gw2_send,
    gw2_recv,
    gp_send,
    gp_recv,
    enc_ref,
    dest_ref,
    label_ref,
    off_ref,
    band_ref,
    w_enc_ref,
    w_dec_ref,
    w_out_ref,
    bias_ref,
    blank_ref,
    cot_ref,
    logp_ref,
    grad_enc_ref,
    grad_pred_ref,
    grad_w_ref,
    dp_sem,
    frame_sem,
    load_sem,
    store_sem,
):
    owners, shards, cap, rows, kept, reduce_here = dims
    me = lax.axis_index("dp")
    part = lax.axis_index("frame")
    width = enc_hbm.shape[1]
    vocab = w_out_hbm.shape[0]
    lab_part = pred_ref.shape[0]
    labels = shards * lab_part
    slots = owners * cap
    f32, bf16 = jnp.float32, jnp.bfloat16

    def iota(shape, dim):
        return lax.broadcasted_iota(jnp.int32, shape, dim)

    def to_owner(step, src, dst, kind):
        peer = lax.rem(me + step, owners)
        return pltpu.make_async_remote_copy(
            src_ref=src(peer),
            dst_ref=dst(step),
            send_sem=dp_sem.at[kind, 0, step],
            recv_sem=dp_sem.at[kind, 1, step],
            device_id={"dp": peer},
            device_id_type=MESH,
        )

    def to_shard(step, src, dst, kind):
        peer = lax.rem(part + step, shards)
        return pltpu.make_async_remote_copy(
            src_ref=src(peer),
            dst_ref=dst(step),
            send_sem=frame_sem.at[kind, 0, step],
            recv_sem=frame_sem.at[kind, 1, step],
            device_id={"frame": peer},
            device_id_type=MESH,
        )

    def each(count, act):
        if count <= 8:
            for step in sorted(range(1, count), key=lambda step: abs(2 * step - count)):
                act(step)
        else:

            def body(step, carry):
                act(step)
                return carry

            lax.fori_loop(1, count, body, 0)

    stores = [
        pltpu.make_async_copy(src, dst, store_sem.at[slot])
        for slot, (src, dst) in enumerate(
            [
                (logp_ref, logp_hbm),
                (grad_pred_ref, grad_pred_hbm),
                (grad_enc_ref, grad_enc_hbm),
                (grad_w_ref, grad_w_hbm),
            ]
        )
    ]

    barrier = pltpu.get_barrier_semaphore()

    def greet_owner(step):
        pl.semaphore_signal(
            barrier, inc=1, device_id={"dp": lax.rem(me + step, owners)}, device_id_type=MESH
        )

    def greet_shard(step):
        pl.semaphore_signal(
            barrier, inc=1, device_id={"frame": lax.rem(part + step, shards)}, device_id_type=MESH
        )

    each(owners, greet_owner)
    each(shards, greet_shard)

    pairs = [
        (dest_hbm, dest_ref),
        (enc_hbm, enc_ref),
        (off_hbm, off_ref),
        (band_hbm, band_ref),
        (blank_hbm, blank_ref),
        (cot_hbm, cot_ref),
        (label_hbm, label_ref),
        (pred_ref, pred_all.at[part]),
        (w_dec_hbm, w_dec_ref),
        (w_enc_hbm, w_enc_ref),
        (w_out_hbm, w_out_ref),
        (bias_hbm, bias_ref),
    ]
    loads = [
        pltpu.make_async_copy(src, dst, load_sem.at[slot]) for slot, (src, dst) in enumerate(pairs)
    ]
    for load in loads:
        load.start()
    loads[0].wait()

    shape = (slots, rows)
    slot_owner = lax.shift_right_logical(iota(shape, 0), log2(cap))
    slot_rank = iota(shape, 0) & (cap - 1)
    lane = iota(shape, 1)
    my_dest = dest_ref[pl.ds(me, 1), :]

    def count(source, sums):
        out_sum, in_sum = sums
        owner_of = lax.shift_right_logical(dest_ref[pl.ds(source, 1), :], log2(rows))
        before_me = (source < me).astype(f32)
        out_sum = out_sum + jnp.where(owner_of == slot_owner, before_me, 0.0)
        mine = jnp.where(owner_of == me, 1.0, 0.0)
        in_sum = in_sum + jnp.where(slot_owner > source, mine, 0.0)
        return out_sum, in_sum

    sums = (jnp.zeros(shape, f32), jnp.zeros(shape, f32))
    if owners <= 8:
        for source in range(owners):
            sums = count(source, sums)
    else:
        sums = lax.fori_loop(0, owners, count, sums)
    out_row = jnp.sum(sums[0], axis=1, keepdims=True).astype(jnp.int32) + slot_rank
    in_row = jnp.sum(sums[1], axis=1, keepdims=True).astype(jnp.int32) + slot_rank
    pick = (my_dest == slot_owner * rows + out_row) & (out_row < rows)
    pick = jnp.where(pick, 1.0, 0.0)
    place = jnp.where(lane == in_row, 1.0, 0.0)
    loads[1].wait()
    out_rows = jnp.dot(pick.astype(bf16), enc_ref[...], preferred_element_type=f32).astype(bf16)
    outbound[...] = out_rows.reshape(owners, cap, width)

    pl.semaphore_wait(barrier, owners - 1 + shards - 1)

    send_enc = functools.partial(
        to_owner, src=lambda peer: outbound.at[peer], dst=lambda step: arrived.at[me], kind=0
    )
    send_pred = functools.partial(
        to_shard, src=lambda peer: pred_ref, dst=lambda step: pred_all.at[part], kind=0
    )
    each(owners, lambda step: send_enc(step).start())
    each(shards, lambda step: send_pred(step).start())
    arrived[me] = outbound[me]
    for load in loads[2:8]:
        load.wait()

    half = iota((1, rows), 1) // BLOCK
    base_row = band_ref[...]
    for block in range(rows // BLOCK):
        base_row = base_row + jnp.where(half == block, off_ref[block], 0)
    cols = jnp.concatenate(
        [
            base_row.astype(f32),
            jnp.zeros((1, rows), f32),
            blank_ref[...],
            cot_ref[...],
        ],
        axis=0,
    ).T
    base_col = cols[:, 0:1].astype(jnp.int32)
    gather_hot = jnp.concatenate(
        [
            jnp.where(iota((rows, labels), 1) == base_col + k, 1.0, 0.0)
            for k in range(kept)
        ],
        axis=0,
    )
    scatter_hot = jnp.concatenate(
        [
            jnp.where(iota((labels, rows), 0) == base_row + k, 1.0, 0.0)
            for k in range(kept)
        ],
        axis=1,
    ).astype(bf16)
    emitted = jnp.sum(gather_hot * label_ref[...].astype(f32), axis=1, keepdims=True)
    emitted = emitted.astype(jnp.int32)
    place_t = place.T.astype(bf16)
    pick_t = pick.T.astype(bf16)
    place = place.astype(bf16)

    each(shards, lambda step: send_pred(step).wait())
    loads[8].wait()
    dec_joint = jnp.dot(
        pred_all[...].reshape(labels, width), w_dec_ref[...], preferred_element_type=f32
    ).astype(bf16)
    dec_rows = jnp.dot(gather_hot.astype(bf16), dec_joint, preferred_element_type=f32)

    for load in loads[9:]:
        load.wait()
    each(owners, lambda step: send_enc(step).wait())
    enc_owned = jnp.dot(
        place_t, arrived[...].reshape(slots, width), preferred_element_type=f32
    ).astype(bf16)
    enc_joint = jnp.dot(enc_owned, w_enc_ref[...], preferred_element_type=f32)
    hidden = jnp.tanh(jnp.concatenate([enc_joint] * kept, axis=0) + dec_rows).astype(bf16)
    logits = (
        lax.dot_general(
            hidden, w_out_ref[...], (((1,), (1,)), ((), ())), preferred_element_type=f32
        )
        + bias_ref[...]
    )
    top = jnp.max(logits, axis=1, keepdims=True)
    shifted = logits - top
    powers = jnp.exp(shifted)
    total = jnp.sum(powers, axis=1, keepdims=True)
    log_total = jnp.log(total)
    word = iota((rows * kept, vocab), 1)
    is_label = word == emitted
    blank_logp = shifted[:, 0:1] - log_total
    label_logp = jnp.sum(jnp.where(is_label, shifted, 0.0), axis=1, keepdims=True) - log_total
    cot_blank = jnp.concatenate([cols[:, 2 + k : 3 + k] for k in range(kept)], axis=0)
    cot_label = jnp.concatenate([cols[:, 2 + kept + k : 3 + kept + k] for k in range(kept)], axis=0)
    scale = (cot_blank + cot_label) / total
    dlogit = (
        jnp.where(word == 0, cot_blank, 0.0) + jnp.where(is_label, cot_label, 0.0) - powers * scale
    ).astype(bf16)

    grad_w = lax.dot_general(
        hidden, dlogit, (((0,), (0,)), ((), ())), preferred_element_type=f32
    ).astype(bf16)
    if reduce_here:
        gw_send[...] = grad_w.reshape(gw_send.shape)
        send_gw = functools.partial(
            to_shard,
            src=lambda peer: gw_send.at[:, peer],
            dst=lambda step: gw_recv.at[step],
            kind=1,
        )
        each(shards, lambda step: send_gw(step).start())
    else:
        grad_w_ref[...] = grad_w.astype(f32)
        stores[3].start()

    back = jnp.dot(dlogit, w_out_ref[...], preferred_element_type=f32)
    hidden_f = hidden.astype(f32)
    dz = back * (1.0 - hidden_f * hidden_f)
    enc_grad = dz[0:rows]
    for k in range(1, kept):
        enc_grad = enc_grad + dz[k * rows : (k + 1) * rows]
    owned_grad = lax.dot_general(
        enc_grad.astype(bf16), w_enc_ref[...], (((1,), (1,)), ((), ())), preferred_element_type=f32
    ).astype(bf16)
    outgoing[...] = (
        jnp.dot(place, owned_grad, preferred_element_type=f32)
        .astype(bf16)
        .reshape(owners, cap, width)
    )
    send_back = functools.partial(
        to_owner, src=lambda peer: outgoing.at[peer], dst=lambda step: returned.at[me], kind=1
    )
    each(owners, lambda step: send_back(step).start())
    returned[me] = outgoing[me]

    dec_grad = jnp.dot(scatter_hot, dz.astype(bf16), preferred_element_type=f32)
    gp_send[...] = (
        lax.dot_general(
            dec_grad.astype(bf16),
            w_dec_ref[...],
            (((1,), (1,)), ((), ())),
            preferred_element_type=f32,
        )
        .astype(bf16)
        .reshape(shards, lab_part, width)
    )
    send_gp = functools.partial(
        to_shard, src=lambda peer: gp_send.at[peer], dst=lambda step: gp_recv.at[step], kind=2
    )
    each(shards, lambda step: send_gp(step).start())

    if reduce_here:
        each(shards, lambda step: send_gw(step).wait())
        owner_sum = gw_send[:, part].astype(f32)
        for step in range(1, shards):
            owner_sum = owner_sum + gw_recv[step].astype(f32)
        gw2_send[...] = owner_sum.astype(bf16)
        send_gw2 = functools.partial(
            to_owner, src=lambda peer: gw2_send.at[peer], dst=lambda step: gw2_recv.at[step], kind=2
        )
        each(owners, lambda step: send_gw2(step).start())

    logp_cols = jnp.concatenate(
        [blank_logp[k * rows : (k + 1) * rows] for k in range(kept)]
        + [label_logp[k * rows : (k + 1) * rows] for k in range(kept)]
        + [jnp.zeros((rows, 8 - 2 * kept), f32)],
        axis=1,
    )
    logp_ref[...] = logp_cols.T[: 2 * kept]
    stores[0].start()

    each(shards, lambda step: send_gp(step).wait())
    pred_sum = gp_send[part].astype(f32)
    for step in range(1, shards):
        pred_sum = pred_sum + gp_recv[step].astype(f32)
    grad_pred_ref[...] = pred_sum
    stores[1].start()

    each(owners, lambda step: send_back(step).wait())
    grad_enc_ref[...] = jnp.dot(
        pick_t, returned[...].reshape(slots, width), preferred_element_type=f32
    ).astype(bf16)
    stores[2].start()

    if reduce_here:
        each(owners, lambda step: send_gw2(step).wait())
        whole_sum = gw2_send[me].astype(f32)
        for step in range(1, owners):
            whole_sum = whole_sum + gw2_recv[step].astype(f32)
        grad_w_ref[...] = whole_sum
        stores[3].start()
    for store in stores:
        store.wait()


def finish_kernel(*refs):
    *ends, sem = refs
    count = len(ends) // 2
    copies = [
        pltpu.make_async_copy(ends[slot], ends[count + slot], sem.at[slot]) for slot in range(count)
    ]
    for copy in copies:
        copy.start()
    for copy in copies:
        copy.wait()


def shards_fn(
    enc_rows,
    dest,
    pred_rows,
    label_ids,
    block_off,
    band_start,
    w_enc,
    w_dec,
    w_out,
    bias_out,
    grad_blank,
    grad_label,
):
    owners = lax.axis_size("dp")
    shards = lax.axis_size("frame")
    rows, width = enc_rows.shape
    kept = grad_blank.shape[1]
    joint = w_enc.shape[1]
    vocab = w_out.shape[1]
    lab_part = pred_rows.shape[0]
    cap = max(TILE_ROWS, 2 * rows // owners)
    per_device = joint // (owners * shards)
    reduce_here = per_device % TILE_ROWS == 0
    grad_rows = per_device if reduce_here else joint
    slot_rows = per_device if reduce_here else TILE_ROWS
    slot_owners = owners if reduce_here else 1
    bf16 = jnp.bfloat16
    hbm = pl.BlockSpec(memory_space=pltpu.HBM)
    exchange = pltpu.VMEM((owners, cap, width), bf16)
    arrays = (
        enc_rows,
        dest[:, 0, :],
        pred_rows,
        label_ids,
        block_off,
        band_start[None, :],
        w_enc,
        w_dec,
        w_out.T,
        bias_out[None, :],
        grad_blank.T,
        grad_label.T,
    )
    fetched = [
        (pltpu.SMEM if slot == 4 else pltpu.VMEM)(array.shape, array.dtype)
        for slot, array in enumerate(arrays)
        if slot != 2
    ]
    outputs = (
        jax.ShapeDtypeStruct((2 * kept, rows), jnp.float32),
        jax.ShapeDtypeStruct((rows, width), bf16),
        jax.ShapeDtypeStruct((lab_part, width), jnp.float32),
        jax.ShapeDtypeStruct((grad_rows, vocab), jnp.float32),
    )
    results = pl.pallas_call(
        functools.partial(joint_kernel, (owners, shards, cap, rows, kept, reduce_here)),
        out_shape=outputs,
        in_specs=[hbm] * len(arrays),
        out_specs=(hbm,) * 4,
        scratch_shapes=[
            exchange,
            exchange,
            exchange,
            exchange,
            pltpu.VMEM((shards, lab_part, width), bf16),
            pltpu.VMEM((slot_owners, shards, slot_rows, vocab), bf16),
            pltpu.VMEM((shards, slot_owners, slot_rows, vocab), bf16),
            pltpu.VMEM((slot_owners, slot_rows, vocab), bf16),
            pltpu.VMEM((slot_owners, slot_rows, vocab), bf16),
            pltpu.VMEM((shards, lab_part, width), bf16),
            pltpu.VMEM((shards, lab_part, width), bf16),
            *fetched,
            *(pltpu.VMEM(output.shape, output.dtype) for output in outputs),
            pltpu.SemaphoreType.DMA((3, 2, owners)),
            pltpu.SemaphoreType.DMA((3, 2, shards)),
            pltpu.SemaphoreType.DMA((len(arrays),)),
            pltpu.SemaphoreType.DMA((len(outputs),)),
        ],
        compiler_params=pltpu.CompilerParams(
            collective_id=0, has_side_effects=True, vmem_limit_bytes=VMEM_BYTES
        ),
    )(*arrays)
    tail = ()
    if not reduce_here:
        *results, grad_w = results
        tail = (lax.psum_scatter(grad_w, ("dp", "frame"), scatter_dimension=0, tiled=True),)
    logp, *others = pl.pallas_call(
        finish_kernel,
        out_shape=tuple(jax.ShapeDtypeStruct(array.shape, array.dtype) for array in results),
        in_specs=[hbm] * len(results),
        out_specs=(hbm,) * len(results),
        scratch_shapes=[pltpu.SemaphoreType.DMA((len(results),))],
        compiler_params=pltpu.CompilerParams(vmem_limit_bytes=VMEM_BYTES),
    )(*results)
    return (logp.T, *others, *tail)


def solution(mesh):
    rows = P(("dp", "frame"), None)
    return jax.shard_map(
        shards_fn,
        mesh=mesh,
        in_specs=(
            rows,
            P(None, "frame", None),
            rows,
            P("dp", None),
            P(("dp", "frame")),
            P(("dp", "frame")),
            P(),
            P(),
            P(),
            P(),
            rows,
            rows,
        ),
        out_specs=(rows, rows, rows, rows),
        check_vma=False,
    )
```

```python
import functools

import jax
import jax.numpy as jnp
from jax import lax
from jax.experimental import pallas as pl
from jax.experimental.pallas import tpu as pltpu
from jax.sharding import PartitionSpec as P

BLOCK = 64
TILE_ROWS = 16
VMEM_BYTES = 64 * 1024 * 1024
MESH = pl.DeviceIdType.MESH


def log2(size):
    assert size & (size - 1) == 0
    return size.bit_length() - 1


def joint_kernel(
    dims,
    enc_hbm,
    dest_hbm,
    pred_ref,
    label_hbm,
    off_hbm,
    band_hbm,
    w_enc_hbm,
    w_dec_hbm,
    w_out_hbm,
    bias_hbm,
    blank_hbm,
    cot_hbm,
    logp_hbm,
    grad_enc_hbm,
    grad_pred_hbm,
    grad_w_hbm,
    outbound,
    arrived,
    outgoing,
    returned,
    pred_all,
    core_send,
    core_recv,
    core_sum,
    first_recv,
    first_sum,
    second_recv,
    last_sum,
    last_recv,
    gp_send,
    gp_recv,
    enc_ref,
    dest_ref,
    label_ref,
    off_ref,
    band_ref,
    w_enc_ref,
    w_dec_ref,
    w_out_ref,
    bias_ref,
    blank_ref,
    cot_ref,
    logp_ref,
    grad_enc_ref,
    grad_pred_ref,
    grad_w_ref,
    dp_sem,
    frame_sem,
    sum_sem,
    load_sem,
    store_sem,
):
    owners, shards, cap, rows, kept, reduce_here = dims
    me = lax.axis_index("dp")
    part = lax.axis_index("frame")
    width = enc_hbm.shape[1]
    vocab = w_out_hbm.shape[0]
    lab_part = pred_ref.shape[0]
    labels = shards * lab_part
    slots = owners * cap
    f32, bf16 = jnp.float32, jnp.bfloat16

    def iota(shape, dim):
        return lax.broadcasted_iota(jnp.int32, shape, dim)

    def to_owner(step, src, dst, kind):
        peer = lax.rem(me + step, owners)
        return pltpu.make_async_remote_copy(
            src_ref=src(peer),
            dst_ref=dst(step),
            send_sem=dp_sem.at[kind, 0, step],
            recv_sem=dp_sem.at[kind, 1, step],
            device_id={"dp": peer},
            device_id_type=MESH,
        )

    def to_shard(step, src, dst, kind):
        peer = lax.rem(part + step, shards)
        return pltpu.make_async_remote_copy(
            src_ref=src(peer),
            dst_ref=dst(step),
            send_sem=frame_sem.at[kind, 0, step],
            recv_sem=frame_sem.at[kind, 1, step],
            device_id={"frame": peer},
            device_id_type=MESH,
        )

    def each(count, act):
        if count <= 8:
            for step in sorted(range(1, count), key=lambda step: abs(2 * step - count)):
                act(step)
        else:

            def body(step, carry):
                act(step)
                return carry

            lax.fori_loop(1, count, body, 0)

    stores = [
        pltpu.make_async_copy(src, dst, store_sem.at[slot])
        for slot, (src, dst) in enumerate(
            [
                (logp_ref, logp_hbm),
                (grad_pred_ref, grad_pred_hbm),
                (grad_enc_ref, grad_enc_hbm),
                (grad_w_ref, grad_w_hbm),
            ]
        )
    ]

    barrier = pltpu.get_barrier_semaphore()

    def greet_owner(step):
        pl.semaphore_signal(
            barrier, inc=1, device_id={"dp": lax.rem(me + step, owners)}, device_id_type=MESH
        )

    def greet_shard(step):
        pl.semaphore_signal(
            barrier, inc=1, device_id={"frame": lax.rem(part + step, shards)}, device_id_type=MESH
        )

    each(owners, greet_owner)
    each(shards, greet_shard)

    pairs = [
        (dest_hbm, dest_ref),
        (enc_hbm, enc_ref),
        (off_hbm, off_ref),
        (band_hbm, band_ref),
        (blank_hbm, blank_ref),
        (cot_hbm, cot_ref),
        (label_hbm, label_ref),
        (pred_ref, pred_all.at[part]),
        (w_dec_hbm, w_dec_ref),
        (w_enc_hbm, w_enc_ref),
        (w_out_hbm, w_out_ref),
        (bias_hbm, bias_ref),
    ]
    loads = [
        pltpu.make_async_copy(src, dst, load_sem.at[slot]) for slot, (src, dst) in enumerate(pairs)
    ]
    for load in loads:
        load.start()
    loads[0].wait()

    shape = (slots, rows)
    slot_owner = lax.shift_right_logical(iota(shape, 0), log2(cap))
    slot_rank = iota(shape, 0) & (cap - 1)
    lane = iota(shape, 1)
    my_dest = dest_ref[pl.ds(me, 1), :]

    def count(source, sums):
        out_sum, in_sum = sums
        owner_of = lax.shift_right_logical(dest_ref[pl.ds(source, 1), :], log2(rows))
        before_me = (source < me).astype(f32)
        out_sum = out_sum + jnp.where(owner_of == slot_owner, before_me, 0.0)
        mine = jnp.where(owner_of == me, 1.0, 0.0)
        in_sum = in_sum + jnp.where(slot_owner > source, mine, 0.0)
        return out_sum, in_sum

    sums = (jnp.zeros(shape, f32), jnp.zeros(shape, f32))
    if owners <= 8:
        for source in range(owners):
            sums = count(source, sums)
    else:
        sums = lax.fori_loop(0, owners, count, sums)
    out_row = jnp.sum(sums[0], axis=1, keepdims=True).astype(jnp.int32) + slot_rank
    in_row = jnp.sum(sums[1], axis=1, keepdims=True).astype(jnp.int32) + slot_rank
    pick = (my_dest == slot_owner * rows + out_row) & (out_row < rows)
    pick = jnp.where(pick, 1.0, 0.0)
    place = jnp.where(lane == in_row, 1.0, 0.0)
    loads[1].wait()
    out_rows = jnp.dot(pick.astype(bf16), enc_ref[...], preferred_element_type=f32).astype(bf16)
    outbound[...] = out_rows.reshape(owners, cap, width)

    pl.semaphore_wait(barrier, owners - 1 + shards - 1)

    send_enc = functools.partial(
        to_owner, src=lambda peer: outbound.at[peer], dst=lambda step: arrived.at[me], kind=0
    )
    send_pred = functools.partial(
        to_shard, src=lambda peer: pred_ref, dst=lambda step: pred_all.at[part], kind=0
    )
    each(owners, lambda step: send_enc(step).start())
    each(shards, lambda step: send_pred(step).start())
    arrived[me] = outbound[me]
    for load in loads[2:8]:
        load.wait()

    half = iota((1, rows), 1) // BLOCK
    base_row = band_ref[...]
    for block in range(rows // BLOCK):
        base_row = base_row + jnp.where(half == block, off_ref[block], 0)
    cols = jnp.concatenate(
        [
            base_row.astype(f32),
            jnp.zeros((1, rows), f32),
            blank_ref[...],
            cot_ref[...],
        ],
        axis=0,
    ).T
    base_col = cols[:, 0:1].astype(jnp.int32)
    gather_hot = jnp.concatenate(
        [
            jnp.where(iota((rows, labels), 1) == base_col + k, 1.0, 0.0)
            for k in range(kept)
        ],
        axis=0,
    )
    scatter_hot = jnp.concatenate(
        [
            jnp.where(iota((labels, rows), 0) == base_row + k, 1.0, 0.0)
            for k in range(kept)
        ],
        axis=1,
    ).astype(bf16)
    emitted = jnp.sum(gather_hot * label_ref[...].astype(f32), axis=1, keepdims=True)
    emitted = emitted.astype(jnp.int32)
    place_t = place.T.astype(bf16)
    pick_t = pick.T.astype(bf16)
    place = place.astype(bf16)

    each(shards, lambda step: send_pred(step).wait())
    loads[8].wait()
    dec_joint = jnp.dot(
        pred_all[...].reshape(labels, width), w_dec_ref[...], preferred_element_type=f32
    ).astype(bf16)
    dec_rows = jnp.dot(gather_hot.astype(bf16), dec_joint, preferred_element_type=f32)

    for load in loads[9:]:
        load.wait()
    each(owners, lambda step: send_enc(step).wait())
    enc_owned = jnp.dot(
        place_t, arrived[...].reshape(slots, width), preferred_element_type=f32
    ).astype(bf16)
    enc_joint = jnp.dot(enc_owned, w_enc_ref[...], preferred_element_type=f32)
    hidden = jnp.tanh(jnp.concatenate([enc_joint] * kept, axis=0) + dec_rows).astype(bf16)
    logits = (
        lax.dot_general(
            hidden, w_out_ref[...], (((1,), (1,)), ((), ())), preferred_element_type=f32
        )
        + bias_ref[...]
    )
    top = jnp.max(logits, axis=1, keepdims=True)
    shifted = logits - top
    powers = jnp.exp(shifted)
    total = jnp.sum(powers, axis=1, keepdims=True)
    log_total = jnp.log(total)
    word = iota((rows * kept, vocab), 1)
    is_label = word == emitted
    blank_logp = shifted[:, 0:1] - log_total
    label_logp = jnp.sum(jnp.where(is_label, shifted, 0.0), axis=1, keepdims=True) - log_total
    cot_blank = jnp.concatenate([cols[:, 2 + k : 3 + k] for k in range(kept)], axis=0)
    cot_label = jnp.concatenate([cols[:, 2 + kept + k : 3 + kept + k] for k in range(kept)], axis=0)
    scale = (cot_blank + cot_label) / total
    dlogit = (
        jnp.where(word == 0, cot_blank, 0.0) + jnp.where(is_label, cot_label, 0.0) - powers * scale
    ).astype(bf16)

    grad_w = lax.dot_general(
        hidden, dlogit, (((0,), (0,)), ((), ())), preferred_element_type=f32
    ).astype(bf16)
    inner, core = lax.rem(me, 2), lax.rem(part, 2)
    outer_at, y = me // 2, part // 2
    outer = owners // 2
    half = outer // 2
    other_core = {"frame": part + 1 - 2 * core}
    other_y = {"frame": lax.rem(part + 2, shards)}
    other_x = {"dp": me + 1 - 2 * inner}

    def send_sum(slot, src, dst, device):
        return pltpu.make_async_remote_copy(
            src_ref=src,
            dst_ref=dst,
            send_sem=sum_sem.at[0, slot],
            recv_sem=sum_sem.at[1, slot],
            device_id=device,
            device_id_type=MESH,
        )

    def add(one, two):
        return (one.astype(f32) + two.astype(f32)).astype(bf16)

    if reduce_here:
        core_send[...] = grad_w.reshape(core_send.shape)
        core_step = send_sum(0, core_send.at[:, :, :, 1 - core], core_recv, other_core)
        core_step.start()
    else:
        grad_w_ref[...] = grad_w.astype(f32)
        stores[3].start()

    back = jnp.dot(dlogit, w_out_ref[...], preferred_element_type=f32)
    hidden_f = hidden.astype(f32)
    dz = back * (1.0 - hidden_f * hidden_f)
    enc_grad = dz[0:rows]
    for k in range(1, kept):
        enc_grad = enc_grad + dz[k * rows : (k + 1) * rows]
    owned_grad = lax.dot_general(
        enc_grad.astype(bf16), w_enc_ref[...], (((1,), (1,)), ((), ())), preferred_element_type=f32
    ).astype(bf16)
    outgoing[...] = (
        jnp.dot(place, owned_grad, preferred_element_type=f32)
        .astype(bf16)
        .reshape(owners, cap, width)
    )
    send_back = functools.partial(
        to_owner, src=lambda peer: outgoing.at[peer], dst=lambda step: returned.at[me], kind=1
    )
    each(owners, lambda step: send_back(step).start())
    returned[me] = outgoing[me]

    if reduce_here:
        core_step.wait()
        core_sum[...] = add(core_send[:, :, :, core], core_recv[...])
        low, high = pl.ds(0, half), pl.ds(half, half)
        first_steps = (
            send_sum(1, core_sum.at[low, :, 1 - y], first_recv.at[0], other_y),
            send_sum(2, core_sum.at[high, 1 - inner], first_recv.at[1], other_x),
        )
        for step in first_steps:
            step.start()

    dec_grad = jnp.dot(scatter_hot, dz.astype(bf16), preferred_element_type=f32)
    gp_send[...] = (
        lax.dot_general(
            dec_grad.astype(bf16),
            w_dec_ref[...],
            (((1,), (1,)), ((), ())),
            preferred_element_type=f32,
        )
        .astype(bf16)
        .reshape(shards, lab_part, width)
    )
    send_gp = functools.partial(
        to_shard, src=lambda peer: gp_send.at[peer], dst=lambda step: gp_recv.at[step], kind=1
    )
    each(shards, lambda step: send_gp(step).start())

    if reduce_here:
        for step in first_steps:
            step.wait()
        first_sum[0] = add(core_sum[low, :, y], first_recv[0])
        first_sum[1] = add(core_sum[high, inner], first_recv[1])
        second_steps = (
            send_sum(3, first_sum.at[0, :, 1 - inner], second_recv.at[0], other_x),
            send_sum(4, first_sum.at[1, :, 1 - y], second_recv.at[1], other_y),
        )
        for step in second_steps:
            step.start()

    logp_cols = jnp.concatenate(
        [blank_logp[k * rows : (k + 1) * rows] for k in range(kept)]
        + [label_logp[k * rows : (k + 1) * rows] for k in range(kept)]
        + [jnp.zeros((rows, 8 - 2 * kept), f32)],
        axis=1,
    )
    logp_ref[...] = logp_cols.T[: 2 * kept]
    stores[0].start()

    if reduce_here:
        for step in second_steps:
            step.wait()
        last_sum[low] = add(first_sum[0, :, inner], second_recv[0])
        last_sum[high] = add(first_sum[1, :, y], second_recv[1])
        last_steps = []
        for step in range(1, outer):
            peer = lax.rem(outer_at + step, outer)
            last_steps.append(
                send_sum(
                    4 + step, last_sum.at[peer], last_recv.at[step], {"dp": 2 * peer + inner}
                )
            )
        for step in last_steps:
            step.start()

    each(shards, lambda step: send_gp(step).wait())
    pred_sum = gp_send[part].astype(f32)
    for step in range(1, shards):
        pred_sum = pred_sum + gp_recv[step].astype(f32)
    grad_pred_ref[...] = pred_sum
    stores[1].start()

    each(owners, lambda step: send_back(step).wait())
    grad_enc_ref[...] = jnp.dot(
        pick_t, returned[...].reshape(slots, width), preferred_element_type=f32
    ).astype(bf16)
    stores[2].start()

    if reduce_here:
        for step in last_steps:
            step.wait()
        whole_sum = last_sum[outer_at].astype(f32)
        for step in range(1, outer):
            whole_sum = whole_sum + last_recv[step].astype(f32)
        grad_w_ref[...] = whole_sum
        stores[3].start()
    for store in stores:
        store.wait()


def finish_kernel(*refs):
    *ends, load_sem, store_sem = refs
    count = len(ends) // 3
    sources, results, held = ends[:count], ends[count : 2 * count], ends[2 * count :]
    loads = [
        pltpu.make_async_copy(sources[slot], held[slot], load_sem.at[slot])
        for slot in range(count)
    ]
    stores = [
        pltpu.make_async_copy(held[slot], results[slot], store_sem.at[slot])
        for slot in range(count)
    ]
    for load in loads:
        load.start()
    for load, store in zip(loads, stores):
        load.wait()
        store.start()
    for store in stores:
        store.wait()


def shards_fn(
    enc_rows,
    dest,
    pred_rows,
    label_ids,
    block_off,
    band_start,
    w_enc,
    w_dec,
    w_out,
    bias_out,
    grad_blank,
    grad_label,
):
    owners = lax.axis_size("dp")
    shards = lax.axis_size("frame")
    rows, width = enc_rows.shape
    kept = grad_blank.shape[1]
    joint = w_enc.shape[1]
    vocab = w_out.shape[1]
    lab_part = pred_rows.shape[0]
    cap = max(TILE_ROWS, 2 * rows // owners)
    per_device = joint // (owners * shards)
    reduce_here = per_device % TILE_ROWS == 0 and owners % 4 == 0 and shards == 4
    grad_rows = per_device if reduce_here else joint
    slot_rows = per_device if reduce_here else TILE_ROWS
    outer = owners // 2 if reduce_here else 2
    half = outer // 2
    bf16 = jnp.bfloat16
    hbm = pl.BlockSpec(memory_space=pltpu.HBM)
    exchange = pltpu.VMEM((owners, cap, width), bf16)
    arrays = (
        enc_rows,
        dest[:, 0, :],
        pred_rows,
        label_ids,
        block_off,
        band_start[None, :],
        w_enc,
        w_dec,
        w_out.T,
        bias_out[None, :],
        grad_blank.T,
        grad_label.T,
    )
    fetched = [
        (pltpu.SMEM if slot == 4 else pltpu.VMEM)(array.shape, array.dtype)
        for slot, array in enumerate(arrays)
        if slot != 2
    ]
    outputs = (
        jax.ShapeDtypeStruct((2 * kept, rows), jnp.float32),
        jax.ShapeDtypeStruct((rows, width), bf16),
        jax.ShapeDtypeStruct((lab_part, width), jnp.float32),
        jax.ShapeDtypeStruct((grad_rows, vocab), jnp.float32),
    )
    results = pl.pallas_call(
        functools.partial(joint_kernel, (owners, shards, cap, rows, kept, reduce_here)),
        out_shape=outputs,
        in_specs=[hbm] * len(arrays),
        out_specs=(hbm,) * 4,
        scratch_shapes=[
            exchange,
            exchange,
            exchange,
            exchange,
            pltpu.VMEM((shards, lab_part, width), bf16),
            pltpu.VMEM((outer, 2, 2, 2, slot_rows, vocab), bf16),
            pltpu.VMEM((outer, 2, 2, slot_rows, vocab), bf16),
            pltpu.VMEM((outer, 2, 2, slot_rows, vocab), bf16),
            pltpu.VMEM((2, half, 2, slot_rows, vocab), bf16),
            pltpu.VMEM((2, half, 2, slot_rows, vocab), bf16),
            pltpu.VMEM((2, half, slot_rows, vocab), bf16),
            pltpu.VMEM((outer, slot_rows, vocab), bf16),
            pltpu.VMEM((outer, slot_rows, vocab), bf16),
            pltpu.VMEM((shards, lab_part, width), bf16),
            pltpu.VMEM((shards, lab_part, width), bf16),
            *fetched,
            *(pltpu.VMEM(output.shape, output.dtype) for output in outputs),
            pltpu.SemaphoreType.DMA((2, 2, owners)),
            pltpu.SemaphoreType.DMA((2, 2, shards)),
            pltpu.SemaphoreType.DMA((2, 5 + outer)),
            pltpu.SemaphoreType.DMA((len(arrays),)),
            pltpu.SemaphoreType.DMA((len(outputs),)),
        ],
        compiler_params=pltpu.CompilerParams(
            collective_id=0, has_side_effects=True, vmem_limit_bytes=VMEM_BYTES
        ),
    )(*arrays)
    tail = ()
    if not reduce_here:
        *results, grad_w = results
        tail = (lax.psum_scatter(grad_w, ("dp", "frame"), scatter_dimension=0, tiled=True),)
    logp, *others = pl.pallas_call(
        finish_kernel,
        out_shape=tuple(jax.ShapeDtypeStruct(array.shape, array.dtype) for array in results),
        in_specs=[hbm] * len(results),
        out_specs=(hbm,) * len(results),
        scratch_shapes=[
            *(pltpu.VMEM(array.shape, array.dtype) for array in results),
            pltpu.SemaphoreType.DMA((len(results),)),
            pltpu.SemaphoreType.DMA((len(results),)),
        ],
        compiler_params=pltpu.CompilerParams(vmem_limit_bytes=VMEM_BYTES),
    )(*results)
    return (logp.T, *others, *tail)


def solution(mesh):
    rows = P(("dp", "frame"), None)
    return jax.shard_map(
        shards_fn,
        mesh=mesh,
        in_specs=(
            rows,
            P(None, "frame", None),
            rows,
            P("dp", None),
            P(("dp", "frame")),
            P(("dp", "frame")),
            P(),
            P(),
            P(),
            P(),
            rows,
            rows,
        ),
        out_specs=(rows, rows, rows, rows),
        check_vma=False,
    )
```

```python
import functools

import jax
import jax.numpy as jnp
from jax import lax
from jax.experimental import pallas as pl
from jax.experimental.pallas import tpu as pltpu
from jax.sharding import PartitionSpec as P

BLOCK = 64
TILE_ROWS = 16
VMEM_BYTES = 64 * 1024 * 1024
MESH = pl.DeviceIdType.MESH


def log2(size):
    assert size & (size - 1) == 0
    return size.bit_length() - 1


def joint_kernel(
    dims,
    enc_hbm,
    dest_hbm,
    pred_ref,
    label_hbm,
    off_hbm,
    band_hbm,
    w_enc_hbm,
    w_dec_hbm,
    w_out_hbm,
    bias_hbm,
    blank_hbm,
    cot_hbm,
    logp_hbm,
    grad_enc_hbm,
    grad_pred_hbm,
    grad_w_hbm,
    outbound,
    arrived,
    outgoing,
    returned,
    pred_all,
    core_send,
    core_recv,
    core_sum,
    first_recv,
    first_sum,
    second_recv,
    last_sum,
    last_recv,
    gp_send,
    gp_recv,
    enc_ref,
    dest_ref,
    label_ref,
    off_ref,
    band_ref,
    w_enc_ref,
    w_dec_ref,
    w_out_ref,
    bias_ref,
    blank_ref,
    cot_ref,
    w_out_t,
    w_enc_t,
    w_dec_t,
    logp_ref,
    grad_enc_ref,
    grad_pred_ref,
    grad_w_ref,
    dp_sem,
    frame_sem,
    sum_sem,
    load_sem,
    store_sem,
):
    owners, shards, cap, rows, kept, reduce_here = dims
    me = lax.axis_index("dp")
    part = lax.axis_index("frame")
    width = enc_hbm.shape[1]
    vocab = w_out_hbm.shape[0]
    lab_part = pred_ref.shape[0]
    labels = shards * lab_part
    slots = owners * cap
    f32, bf16 = jnp.float32, jnp.bfloat16

    def iota(shape, dim):
        return lax.broadcasted_iota(jnp.int32, shape, dim)

    def to_owner(step, src, dst, kind):
        peer = lax.rem(me + step, owners)
        return pltpu.make_async_remote_copy(
            src_ref=src(peer),
            dst_ref=dst(step),
            send_sem=dp_sem.at[kind, 0, step],
            recv_sem=dp_sem.at[kind, 1, step],
            device_id={"dp": peer},
            device_id_type=MESH,
        )

    def to_shard(step, src, dst, kind):
        peer = lax.rem(part + step, shards)
        return pltpu.make_async_remote_copy(
            src_ref=src(peer),
            dst_ref=dst(step),
            send_sem=frame_sem.at[kind, 0, step],
            recv_sem=frame_sem.at[kind, 1, step],
            device_id={"frame": peer},
            device_id_type=MESH,
        )

    def each(count, act):
        if count <= 8:
            for step in sorted(range(1, count), key=lambda step: abs(2 * step - count)):
                act(step)
        else:

            def body(step, carry):
                act(step)
                return carry

            lax.fori_loop(1, count, body, 0)

    stores = [
        pltpu.make_async_copy(src, dst, store_sem.at[slot])
        for slot, (src, dst) in enumerate(
            [
                (logp_ref, logp_hbm),
                (grad_pred_ref, grad_pred_hbm),
                (grad_enc_ref, grad_enc_hbm),
                (grad_w_ref, grad_w_hbm),
            ]
        )
    ]

    barrier = pltpu.get_barrier_semaphore()

    def greet_owner(step):
        pl.semaphore_signal(
            barrier, inc=1, device_id={"dp": lax.rem(me + step, owners)}, device_id_type=MESH
        )

    def greet_shard(step):
        pl.semaphore_signal(
            barrier, inc=1, device_id={"frame": lax.rem(part + step, shards)}, device_id_type=MESH
        )

    each(owners, greet_owner)
    each(shards, greet_shard)

    pairs = [
        (dest_hbm, dest_ref),
        (enc_hbm, enc_ref),
        (off_hbm, off_ref),
        (band_hbm, band_ref),
        (blank_hbm, blank_ref),
        (cot_hbm, cot_ref),
        (label_hbm, label_ref),
        (pred_ref, pred_all.at[part]),
        (w_dec_hbm, w_dec_ref),
        (w_enc_hbm, w_enc_ref),
        (w_out_hbm, w_out_ref),
        (bias_hbm, bias_ref),
    ]
    loads = [
        pltpu.make_async_copy(src, dst, load_sem.at[slot]) for slot, (src, dst) in enumerate(pairs)
    ]
    for load in loads:
        load.start()
    loads[0].wait()

    shape = (slots, rows)
    slot_owner = lax.shift_right_logical(iota(shape, 0), log2(cap))
    slot_rank = iota(shape, 0) & (cap - 1)
    lane = iota(shape, 1)
    my_dest = dest_ref[pl.ds(me, 1), :]

    def count(source, sums):
        out_sum, in_sum = sums
        owner_of = lax.shift_right_logical(dest_ref[pl.ds(source, 1), :], log2(rows))
        before_me = (source < me).astype(f32)
        out_sum = out_sum + jnp.where(owner_of == slot_owner, before_me, 0.0)
        mine = jnp.where(owner_of == me, 1.0, 0.0)
        in_sum = in_sum + jnp.where(slot_owner > source, mine, 0.0)
        return out_sum, in_sum

    sums = (jnp.zeros(shape, f32), jnp.zeros(shape, f32))
    if owners <= 8:
        for source in range(owners):
            sums = count(source, sums)
    else:
        sums = lax.fori_loop(0, owners, count, sums)
    out_row = jnp.sum(sums[0], axis=1, keepdims=True).astype(jnp.int32) + slot_rank
    in_row = jnp.sum(sums[1], axis=1, keepdims=True).astype(jnp.int32) + slot_rank
    pick = (my_dest == slot_owner * rows + out_row) & (out_row < rows)
    pick = jnp.where(pick, 1.0, 0.0)
    place = jnp.where(lane == in_row, 1.0, 0.0)
    loads[1].wait()
    out_rows = jnp.dot(pick.astype(bf16), enc_ref[...], preferred_element_type=f32).astype(bf16)
    outbound[...] = out_rows.reshape(owners, cap, width)

    pl.semaphore_wait(barrier, owners - 1 + shards - 1)

    send_enc = functools.partial(
        to_owner, src=lambda peer: outbound.at[peer], dst=lambda step: arrived.at[me], kind=0
    )
    send_pred = functools.partial(
        to_shard, src=lambda peer: pred_ref, dst=lambda step: pred_all.at[part], kind=0
    )
    each(owners, lambda step: send_enc(step).start())
    each(shards, lambda step: send_pred(step).start())
    arrived[me] = outbound[me]
    for load in loads[2:8]:
        load.wait()

    half = iota((1, rows), 1) // BLOCK
    base_row = band_ref[...]
    for block in range(rows // BLOCK):
        base_row = base_row + jnp.where(half == block, off_ref[block], 0)
    cols = jnp.concatenate(
        [
            base_row.astype(f32),
            jnp.zeros((1, rows), f32),
            blank_ref[...],
            cot_ref[...],
        ],
        axis=0,
    ).T
    base_col = cols[:, 0:1].astype(jnp.int32)
    gather_hot = jnp.concatenate(
        [
            jnp.where(iota((rows, labels), 1) == base_col + k, 1.0, 0.0)
            for k in range(kept)
        ],
        axis=0,
    )
    scatter_hot = jnp.concatenate(
        [
            jnp.where(iota((labels, rows), 0) == base_row + k, 1.0, 0.0)
            for k in range(kept)
        ],
        axis=1,
    ).astype(bf16)
    emitted = jnp.sum(gather_hot * label_ref[...].astype(f32), axis=1, keepdims=True)
    emitted = emitted.astype(jnp.int32)
    place_t = place.T.astype(bf16)
    pick_t = pick.T.astype(bf16)
    place = place.astype(bf16)

    each(shards, lambda step: send_pred(step).wait())
    loads[8].wait()
    dec_joint = jnp.dot(
        pred_all[...].reshape(labels, width), w_dec_ref[...], preferred_element_type=f32
    ).astype(bf16)
    dec_rows = jnp.dot(gather_hot.astype(bf16), dec_joint, preferred_element_type=f32)

    for load in loads[9:]:
        load.wait()
    w_out_t[...] = w_out_ref[...].T
    w_enc_t[...] = w_enc_ref[...].T
    w_dec_t[...] = w_dec_ref[...].T
    each(owners, lambda step: send_enc(step).wait())
    enc_owned = jnp.dot(
        place_t, arrived[...].reshape(slots, width), preferred_element_type=f32
    ).astype(bf16)
    enc_joint = jnp.dot(enc_owned, w_enc_ref[...], preferred_element_type=f32)
    word = iota((rows, vocab), 1)
    hiddens, hiddens_t, dlogits, blank_logps, label_logps = [], [], [], [], []
    for k in range(kept):
        span = slice(k * rows, (k + 1) * rows)
        hidden = jnp.tanh(enc_joint + dec_rows[span]).astype(bf16)
        logits = jnp.dot(hidden, w_out_t[...], preferred_element_type=f32) + bias_ref[...]
        hiddens.append(hidden)
        hiddens_t.append(hidden.T)
        shifted = logits - jnp.max(logits, axis=1, keepdims=True)
        powers = jnp.exp(shifted)
        total = jnp.sum(powers, axis=1, keepdims=True)
        log_total = jnp.log(total)
        is_label = word == emitted[span]
        blank_logps.append(shifted[:, 0:1] - log_total)
        label_logps.append(
            jnp.sum(jnp.where(is_label, shifted, 0.0), axis=1, keepdims=True) - log_total
        )
        cot_blank = cols[:, 2 + k : 3 + k]
        cot_label = cols[:, 2 + kept + k : 3 + kept + k]
        scale = (cot_blank + cot_label) / total
        dlogits.append(
            (
                jnp.where(word == 0, cot_blank, 0.0)
                + jnp.where(is_label, cot_label, 0.0)
                - powers * scale
            ).astype(bf16)
        )

    grad_w = jnp.dot(
        jnp.concatenate(hiddens_t, axis=1),
        jnp.concatenate(dlogits, axis=0),
        preferred_element_type=f32,
    ).astype(bf16)
    inner, core = lax.rem(me, 2), lax.rem(part, 2)
    outer_at, y = me // 2, part // 2
    outer = owners // 2
    half = outer // 2
    other_core = {"frame": part + 1 - 2 * core}
    other_y = {"frame": lax.rem(part + 2, shards)}
    other_x = {"dp": me + 1 - 2 * inner}

    def send_sum(slot, src, dst, device):
        return pltpu.make_async_remote_copy(
            src_ref=src,
            dst_ref=dst,
            send_sem=sum_sem.at[0, slot],
            recv_sem=sum_sem.at[1, slot],
            device_id=device,
            device_id_type=MESH,
        )

    def add(one, two):
        return (one.astype(f32) + two.astype(f32)).astype(bf16)

    if reduce_here:
        core_send[...] = grad_w.reshape(core_send.shape)
        core_steps = [
            send_sum(4 + outer + at, core_send.at[at, :, :, 1 - core], core_recv.at[at], other_core)
            for at in range(outer)
        ]
        for step in core_steps:
            step.start()
    else:
        grad_w_ref[...] = grad_w.astype(f32)
        stores[3].start()

    dzs = []
    for k in range(kept):
        back = jnp.dot(dlogits[k], w_out_ref[...], preferred_element_type=f32)
        hidden_f = hiddens[k].astype(f32)
        dzs.append(back * (1.0 - hidden_f * hidden_f))
    enc_grad = dzs[0]
    for dz in dzs[1:]:
        enc_grad = enc_grad + dz
    owned_grad = lax.dot_general(
        enc_grad.astype(bf16), w_enc_t[...], (((1,), (0,)), ((), ())), preferred_element_type=f32
    ).astype(bf16)
    outgoing[...] = (
        jnp.dot(place, owned_grad, preferred_element_type=f32)
        .astype(bf16)
        .reshape(owners, cap, width)
    )
    send_back = functools.partial(
        to_owner, src=lambda peer: outgoing.at[peer], dst=lambda step: returned.at[me], kind=1
    )
    each(owners, lambda step: send_back(step).start())
    returned[me] = outgoing[me]

    if reduce_here:
        low, high = pl.ds(0, half), pl.ds(half, half)
        first_steps = (
            send_sum(0, core_sum.at[low, :, 1 - y], first_recv.at[0], other_y),
            send_sum(1, core_sum.at[high, 1 - inner], first_recv.at[1], other_x),
        )
        for part_at, blocks in enumerate((low, high)):
            for step in core_steps[part_at * half : (part_at + 1) * half]:
                step.wait()
            core_sum[blocks] = add(core_send[blocks, :, :, core], core_recv[blocks])
            first_steps[part_at].start()

    dz_rows = jnp.concatenate([dz.astype(bf16) for dz in dzs], axis=0)
    dec_grad = jnp.dot(scatter_hot, dz_rows, preferred_element_type=f32)
    gp_send[...] = (
        lax.dot_general(
            dec_grad.astype(bf16),
            w_dec_t[...],
            (((1,), (0,)), ((), ())),
            preferred_element_type=f32,
        )
        .astype(bf16)
        .reshape(shards, lab_part, width)
    )
    send_gp = functools.partial(
        to_shard, src=lambda peer: gp_send.at[peer], dst=lambda step: gp_recv.at[step], kind=1
    )
    each(shards, lambda step: send_gp(step).start())

    if reduce_here:
        second_steps = (
            send_sum(2, first_sum.at[0, :, 1 - inner], second_recv.at[0], other_x),
            send_sum(3, first_sum.at[1, :, 1 - y], second_recv.at[1], other_y),
        )
        kept_blocks = (core_sum.at[low, :, y], core_sum.at[high, inner])
        for part_at in range(2):
            first_steps[part_at].wait()
            first_sum[part_at] = add(kept_blocks[part_at][...], first_recv[part_at])
            second_steps[part_at].start()

    logp_cols = jnp.concatenate(
        blank_logps + label_logps + [jnp.zeros((rows, 8 - 2 * kept), f32)], axis=1
    )
    logp_ref[...] = logp_cols.T[: 2 * kept]
    stores[0].start()

    if reduce_here:
        for step in second_steps:
            step.wait()
        last_sum[low] = add(first_sum[0, :, inner], second_recv[0])
        last_sum[high] = add(first_sum[1, :, y], second_recv[1])
        last_steps = []
        for step in range(1, outer):
            peer = lax.rem(outer_at + step, outer)
            last_steps.append(
                send_sum(
                    3 + step, last_sum.at[peer], last_recv.at[step], {"dp": 2 * peer + inner}
                )
            )
        for step in last_steps:
            step.start()

    each(shards, lambda step: send_gp(step).wait())
    pred_sum = gp_send[part].astype(f32)
    for step in range(1, shards):
        pred_sum = pred_sum + gp_recv[step].astype(f32)
    grad_pred_ref[...] = pred_sum
    stores[1].start()

    each(owners, lambda step: send_back(step).wait())
    grad_enc_ref[...] = jnp.dot(
        pick_t, returned[...].reshape(slots, width), preferred_element_type=f32
    ).astype(bf16)
    stores[2].start()

    if reduce_here:
        for step in last_steps:
            step.wait()
        whole_sum = last_sum[outer_at].astype(f32)
        for step in range(1, outer):
            whole_sum = whole_sum + last_recv[step].astype(f32)
        grad_w_ref[...] = whole_sum
        stores[3].start()
    for store in stores:
        store.wait()


def finish_kernel(*refs):
    *ends, load_sem, store_sem = refs
    count = len(ends) // 3
    sources, results, held = ends[:count], ends[count : 2 * count], ends[2 * count :]
    loads = [
        pltpu.make_async_copy(sources[slot], held[slot], load_sem.at[slot])
        for slot in range(count)
    ]
    stores = [
        pltpu.make_async_copy(held[slot], results[slot], store_sem.at[slot])
        for slot in range(count)
    ]
    for load in loads:
        load.start()
    for load, store in zip(loads, stores):
        load.wait()
        store.start()
    for store in stores:
        store.wait()


def shards_fn(
    enc_rows,
    dest,
    pred_rows,
    label_ids,
    block_off,
    band_start,
    w_enc,
    w_dec,
    w_out,
    bias_out,
    grad_blank,
    grad_label,
):
    owners = lax.axis_size("dp")
    shards = lax.axis_size("frame")
    rows, width = enc_rows.shape
    kept = grad_blank.shape[1]
    joint = w_enc.shape[1]
    vocab = w_out.shape[1]
    lab_part = pred_rows.shape[0]
    cap = max(TILE_ROWS, 2 * rows // owners)
    per_device = joint // (owners * shards)
    reduce_here = per_device % TILE_ROWS == 0 and owners % 4 == 0 and shards == 4
    grad_rows = per_device if reduce_here else joint
    slot_rows = per_device if reduce_here else TILE_ROWS
    outer = owners // 2 if reduce_here else 2
    half = outer // 2
    bf16 = jnp.bfloat16
    hbm = pl.BlockSpec(memory_space=pltpu.HBM)
    exchange = pltpu.VMEM((owners, cap, width), bf16)
    arrays = (
        enc_rows,
        dest[:, 0, :],
        pred_rows,
        label_ids,
        block_off,
        band_start[None, :],
        w_enc,
        w_dec,
        w_out.T,
        bias_out[None, :],
        grad_blank.T,
        grad_label.T,
    )
    fetched = [
        (pltpu.SMEM if slot == 4 else pltpu.VMEM)(array.shape, array.dtype)
        for slot, array in enumerate(arrays)
        if slot != 2
    ]
    outputs = (
        jax.ShapeDtypeStruct((2 * kept, rows), jnp.float32),
        jax.ShapeDtypeStruct((rows, width), bf16),
        jax.ShapeDtypeStruct((lab_part, width), jnp.float32),
        jax.ShapeDtypeStruct((grad_rows, vocab), jnp.float32),
    )
    results = pl.pallas_call(
        functools.partial(joint_kernel, (owners, shards, cap, rows, kept, reduce_here)),
        out_shape=outputs,
        in_specs=[hbm] * len(arrays),
        out_specs=(hbm,) * 4,
        scratch_shapes=[
            exchange,
            exchange,
            exchange,
            exchange,
            pltpu.VMEM((shards, lab_part, width), bf16),
            pltpu.VMEM((outer, 2, 2, 2, slot_rows, vocab), bf16),
            pltpu.VMEM((outer, 2, 2, slot_rows, vocab), bf16),
            pltpu.VMEM((outer, 2, 2, slot_rows, vocab), bf16),
            pltpu.VMEM((2, half, 2, slot_rows, vocab), bf16),
            pltpu.VMEM((2, half, 2, slot_rows, vocab), bf16),
            pltpu.VMEM((2, half, slot_rows, vocab), bf16),
            pltpu.VMEM((outer, slot_rows, vocab), bf16),
            pltpu.VMEM((outer, slot_rows, vocab), bf16),
            pltpu.VMEM((shards, lab_part, width), bf16),
            pltpu.VMEM((shards, lab_part, width), bf16),
            *fetched,
            pltpu.VMEM(w_out.shape, bf16),
            pltpu.VMEM(w_enc.shape[::-1], bf16),
            pltpu.VMEM(w_dec.shape[::-1], bf16),
            *(pltpu.VMEM(output.shape, output.dtype) for output in outputs),
            pltpu.SemaphoreType.DMA((2, 2, owners)),
            pltpu.SemaphoreType.DMA((2, 2, shards)),
            pltpu.SemaphoreType.DMA((2, 4 + 2 * outer)),
            pltpu.SemaphoreType.DMA((len(arrays),)),
            pltpu.SemaphoreType.DMA((len(outputs),)),
        ],
        compiler_params=pltpu.CompilerParams(
            collective_id=0, has_side_effects=True, vmem_limit_bytes=VMEM_BYTES
        ),
    )(*arrays)
    tail = ()
    if not reduce_here:
        *results, grad_w = results
        tail = (lax.psum_scatter(grad_w, ("dp", "frame"), scatter_dimension=0, tiled=True),)
    logp, *others = pl.pallas_call(
        finish_kernel,
        out_shape=tuple(jax.ShapeDtypeStruct(array.shape, array.dtype) for array in results),
        in_specs=[hbm] * len(results),
        out_specs=(hbm,) * len(results),
        scratch_shapes=[
            *(pltpu.VMEM(array.shape, array.dtype) for array in results),
            pltpu.SemaphoreType.DMA((len(results),)),
            pltpu.SemaphoreType.DMA((len(results),)),
        ],
        compiler_params=pltpu.CompilerParams(vmem_limit_bytes=VMEM_BYTES),
    )(*results)
    return (logp.T, *others, *tail)


def solution(mesh):
    rows = P(("dp", "frame"), None)
    return jax.shard_map(
        shards_fn,
        mesh=mesh,
        in_specs=(
            rows,
            P(None, "frame", None),
            rows,
            P("dp", None),
            P(("dp", "frame")),
            P(("dp", "frame")),
            P(),
            P(),
            P(),
            P(),
            rows,
            rows,
        ),
        out_specs=(rows, rows, rows, rows),
        check_vma=False,
    )
```

```python
import functools

import jax
import jax.numpy as jnp
from jax import lax
from jax.experimental import pallas as pl
from jax.experimental.pallas import tpu as pltpu
from jax.sharding import PartitionSpec as P

BLOCK = 64
TILE_ROWS = 16
VMEM_BYTES = 64 * 1024 * 1024
MESH = pl.DeviceIdType.MESH


def log2(size):
    assert size & (size - 1) == 0
    return size.bit_length() - 1


def joint_kernel(
    dims,
    enc_hbm,
    dest_hbm,
    pred_ref,
    label_hbm,
    off_hbm,
    band_hbm,
    w_enc_hbm,
    w_dec_hbm,
    w_out_hbm,
    bias_hbm,
    blank_hbm,
    cot_hbm,
    logp_hbm,
    grad_enc_hbm,
    grad_pred_hbm,
    grad_w_hbm,
    outbound,
    arrived,
    outgoing,
    returned,
    pred_all,
    piece_send,
    piece_recv,
    owner_sum,
    owner_recv,
    gp_send,
    gp_recv,
    enc_ref,
    dest_ref,
    label_ref,
    off_ref,
    band_ref,
    w_enc_ref,
    w_dec_ref,
    w_out_ref,
    bias_ref,
    blank_ref,
    cot_ref,
    w_out_t,
    w_enc_t,
    w_dec_t,
    logp_ref,
    grad_enc_ref,
    grad_pred_ref,
    grad_w_ref,
    dp_sem,
    frame_sem,
    piece_sem,
    owner_sem,
    load_sem,
    store_sem,
):
    owners, shards, cap, rows, kept, reduce_here = dims
    me = lax.axis_index("dp")
    part = lax.axis_index("frame")
    width = enc_hbm.shape[1]
    vocab = w_out_hbm.shape[0]
    lab_part = pred_ref.shape[0]
    labels = shards * lab_part
    slots = owners * cap
    f32, bf16 = jnp.float32, jnp.bfloat16

    def iota(shape, dim):
        return lax.broadcasted_iota(jnp.int32, shape, dim)

    def to_owner(step, src, dst, kind):
        peer = lax.rem(me + step, owners)
        return pltpu.make_async_remote_copy(
            src_ref=src(peer),
            dst_ref=dst(step),
            send_sem=dp_sem.at[kind, 0, step],
            recv_sem=dp_sem.at[kind, 1, step],
            device_id={"dp": peer},
            device_id_type=MESH,
        )

    def to_shard(step, src, dst, kind):
        peer = lax.rem(part + step, shards)
        return pltpu.make_async_remote_copy(
            src_ref=src(peer),
            dst_ref=dst(step),
            send_sem=frame_sem.at[kind, 0, step],
            recv_sem=frame_sem.at[kind, 1, step],
            device_id={"frame": peer},
            device_id_type=MESH,
        )

    def each(count, act):
        if count <= 8:
            for step in sorted(range(1, count), key=lambda step: abs(2 * step - count)):
                act(step)
        else:

            def body(step, carry):
                act(step)
                return carry

            lax.fori_loop(1, count, body, 0)

    stores = [
        pltpu.make_async_copy(src, dst, store_sem.at[slot])
        for slot, (src, dst) in enumerate(
            [
                (logp_ref, logp_hbm),
                (grad_pred_ref, grad_pred_hbm),
                (grad_enc_ref, grad_enc_hbm),
                (grad_w_ref, grad_w_hbm),
            ]
        )
    ]

    barrier = pltpu.get_barrier_semaphore()

    def greet_owner(step):
        pl.semaphore_signal(
            barrier, inc=1, device_id={"dp": lax.rem(me + step, owners)}, device_id_type=MESH
        )

    def greet_shard(step):
        pl.semaphore_signal(
            barrier, inc=1, device_id={"frame": lax.rem(part + step, shards)}, device_id_type=MESH
        )

    each(owners, greet_owner)
    each(shards, greet_shard)

    pairs = [
        (dest_hbm, dest_ref),
        (enc_hbm, enc_ref),
        (off_hbm, off_ref),
        (band_hbm, band_ref),
        (blank_hbm, blank_ref),
        (cot_hbm, cot_ref),
        (label_hbm, label_ref),
        (pred_ref, pred_all.at[part]),
        (w_dec_hbm, w_dec_ref),
        (w_enc_hbm, w_enc_ref),
        (w_out_hbm, w_out_ref),
        (bias_hbm, bias_ref),
    ]
    loads = [
        pltpu.make_async_copy(src, dst, load_sem.at[slot]) for slot, (src, dst) in enumerate(pairs)
    ]
    for load in loads:
        load.start()
    loads[0].wait()

    shape = (slots, rows)
    slot_owner = lax.shift_right_logical(iota(shape, 0), log2(cap))
    slot_rank = iota(shape, 0) & (cap - 1)
    lane = iota(shape, 1)
    my_dest = dest_ref[pl.ds(me, 1), :]

    def count(source, sums):
        out_sum, in_sum = sums
        owner_of = lax.shift_right_logical(dest_ref[pl.ds(source, 1), :], log2(rows))
        before_me = (source < me).astype(f32)
        out_sum = out_sum + jnp.where(owner_of == slot_owner, before_me, 0.0)
        mine = jnp.where(owner_of == me, 1.0, 0.0)
        in_sum = in_sum + jnp.where(slot_owner > source, mine, 0.0)
        return out_sum, in_sum

    sums = (jnp.zeros(shape, f32), jnp.zeros(shape, f32))
    if owners <= 8:
        for source in range(owners):
            sums = count(source, sums)
    else:
        sums = lax.fori_loop(0, owners, count, sums)
    out_row = jnp.sum(sums[0], axis=1, keepdims=True).astype(jnp.int32) + slot_rank
    in_row = jnp.sum(sums[1], axis=1, keepdims=True).astype(jnp.int32) + slot_rank
    pick = (my_dest == slot_owner * rows + out_row) & (out_row < rows)
    pick = jnp.where(pick, 1.0, 0.0)
    place = jnp.where(lane == in_row, 1.0, 0.0)
    loads[1].wait()
    out_rows = jnp.dot(pick.astype(bf16), enc_ref[...], preferred_element_type=f32).astype(bf16)
    outbound[...] = out_rows.reshape(owners, cap, width)

    pl.semaphore_wait(barrier, owners - 1 + shards - 1)

    send_enc = functools.partial(
        to_owner, src=lambda peer: outbound.at[peer], dst=lambda step: arrived.at[me], kind=0
    )
    send_pred = functools.partial(
        to_shard, src=lambda peer: pred_ref, dst=lambda step: pred_all.at[part], kind=0
    )
    each(owners, lambda step: send_enc(step).start())
    each(shards, lambda step: send_pred(step).start())
    arrived[me] = outbound[me]
    for load in loads[2:8]:
        load.wait()

    half = iota((1, rows), 1) // BLOCK
    base_row = band_ref[...]
    for block in range(rows // BLOCK):
        base_row = base_row + jnp.where(half == block, off_ref[block], 0)
    cols = jnp.concatenate(
        [
            base_row.astype(f32),
            jnp.zeros((1, rows), f32),
            blank_ref[...],
            cot_ref[...],
        ],
        axis=0,
    ).T
    base_col = cols[:, 0:1].astype(jnp.int32)
    gather_hot = jnp.concatenate(
        [
            jnp.where(iota((rows, labels), 1) == base_col + k, 1.0, 0.0)
            for k in range(kept)
        ],
        axis=0,
    )
    scatter_hot = jnp.concatenate(
        [
            jnp.where(iota((labels, rows), 0) == base_row + k, 1.0, 0.0)
            for k in range(kept)
        ],
        axis=1,
    ).astype(bf16)
    emitted = jnp.sum(gather_hot * label_ref[...].astype(f32), axis=1, keepdims=True)
    emitted = emitted.astype(jnp.int32)
    place_t = place.T.astype(bf16)
    pick_t = pick.T.astype(bf16)
    place = place.astype(bf16)

    each(shards, lambda step: send_pred(step).wait())
    loads[8].wait()
    dec_joint = jnp.dot(
        pred_all[...].reshape(labels, width), w_dec_ref[...], preferred_element_type=f32
    ).astype(bf16)
    dec_rows = jnp.dot(gather_hot.astype(bf16), dec_joint, preferred_element_type=f32)

    for load in loads[9:]:
        load.wait()
    w_out_t[...] = w_out_ref[...].T
    w_enc_t[...] = w_enc_ref[...].T
    w_dec_t[...] = w_dec_ref[...].T
    each(owners, lambda step: send_enc(step).wait())
    enc_owned = jnp.dot(
        place_t, arrived[...].reshape(slots, width), preferred_element_type=f32
    ).astype(bf16)
    enc_joint = jnp.dot(enc_owned, w_enc_ref[...], preferred_element_type=f32)
    word = iota((rows, vocab), 1)
    hiddens, hiddens_t, dlogits, blank_logps, label_logps = [], [], [], [], []
    for k in range(kept):
        span = slice(k * rows, (k + 1) * rows)
        hidden = jnp.tanh(enc_joint + dec_rows[span]).astype(bf16)
        logits = jnp.dot(hidden, w_out_t[...], preferred_element_type=f32) + bias_ref[...]
        hiddens.append(hidden)
        hiddens_t.append(hidden.T)
        shifted = logits - jnp.max(logits, axis=1, keepdims=True)
        powers = jnp.exp(shifted)
        total = jnp.sum(powers, axis=1, keepdims=True)
        log_total = jnp.log(total)
        is_label = word == emitted[span]
        blank_logps.append(shifted[:, 0:1] - log_total)
        label_logps.append(
            jnp.sum(jnp.where(is_label, shifted, 0.0), axis=1, keepdims=True) - log_total
        )
        cot_blank = cols[:, 2 + k : 3 + k]
        cot_label = cols[:, 2 + kept + k : 3 + kept + k]
        scale = (cot_blank + cot_label) / total
        dlogits.append(
            (
                jnp.where(word == 0, cot_blank, 0.0)
                + jnp.where(is_label, cot_label, 0.0)
                - powers * scale
            ).astype(bf16)
        )

    grad_w = jnp.dot(
        jnp.concatenate(hiddens_t, axis=1),
        jnp.concatenate(dlogits, axis=0),
        preferred_element_type=f32,
    ).astype(bf16)
    inner, outer_at, outer = lax.rem(me, 2), me // 2, owners // 2
    ahead = sorted(range(outer), key=lambda step: (step == 0, abs(2 * step - outer)))

    def piece_copy(near, step):
        peer = lax.rem(part + step, shards)
        return pltpu.make_async_remote_copy(
            src_ref=piece_send.at[lax.rem(outer_at + near, outer), :, peer],
            dst_ref=piece_recv.at[near, step],
            send_sem=piece_sem.at[0, near, step],
            recv_sem=piece_sem.at[1, near, step],
            device_id={"frame": peer},
            device_id_type=MESH,
        )

    def owner_copy(near, side):
        to_inner = lax.rem(inner + side, 2)
        return pltpu.make_async_remote_copy(
            src_ref=owner_sum.at[near, to_inner],
            dst_ref=owner_recv.at[near, side],
            send_sem=owner_sem.at[0, near, side],
            recv_sem=owner_sem.at[1, near, side],
            device_id={"dp": 2 * lax.rem(outer_at + near, outer) + to_inner},
            device_id_type=MESH,
        )

    if reduce_here:
        piece_send[...] = grad_w.reshape(piece_send.shape)
        for near in ahead:
            for step in range(1, shards):
                piece_copy(near, step).start()
    else:
        grad_w_ref[...] = grad_w.astype(f32)
        stores[3].start()

    dzs = []
    for k in range(kept):
        back = jnp.dot(dlogits[k], w_out_ref[...], preferred_element_type=f32)
        hidden_f = hiddens[k].astype(f32)
        dzs.append(back * (1.0 - hidden_f * hidden_f))
    enc_grad = dzs[0]
    for dz in dzs[1:]:
        enc_grad = enc_grad + dz
    owned_grad = lax.dot_general(
        enc_grad.astype(bf16), w_enc_t[...], (((1,), (0,)), ((), ())), preferred_element_type=f32
    ).astype(bf16)
    outgoing[...] = (
        jnp.dot(place, owned_grad, preferred_element_type=f32)
        .astype(bf16)
        .reshape(owners, cap, width)
    )
    send_back = functools.partial(
        to_owner, src=lambda peer: outgoing.at[peer], dst=lambda step: returned.at[me], kind=1
    )
    each(owners, lambda step: send_back(step).start())
    returned[me] = outgoing[me]

    dz_rows = jnp.concatenate([dz.astype(bf16) for dz in dzs], axis=0)
    dec_grad = jnp.dot(scatter_hot, dz_rows, preferred_element_type=f32)
    gp_send[...] = (
        lax.dot_general(
            dec_grad.astype(bf16),
            w_dec_t[...],
            (((1,), (0,)), ((), ())),
            preferred_element_type=f32,
        )
        .astype(bf16)
        .reshape(shards, lab_part, width)
    )
    send_gp = functools.partial(
        to_shard, src=lambda peer: gp_send.at[peer], dst=lambda step: gp_recv.at[step], kind=1
    )
    each(shards, lambda step: send_gp(step).start())

    if reduce_here:
        for near in ahead:
            for step in range(1, shards):
                piece_copy(near, step).wait()
            piece = piece_send[lax.rem(outer_at + near, outer), :, part].astype(f32)
            for step in range(1, shards):
                piece = piece + piece_recv[near, step].astype(f32)
            owner_sum[near] = piece.astype(bf16)
            for side in range(near == 0, 2):
                owner_copy(near, side).start()

    logp_cols = jnp.concatenate(
        blank_logps + label_logps + [jnp.zeros((rows, 8 - 2 * kept), f32)], axis=1
    )
    logp_ref[...] = logp_cols.T[: 2 * kept]
    stores[0].start()

    each(shards, lambda step: send_gp(step).wait())
    pred_sum = gp_send[part].astype(f32)
    for step in range(1, shards):
        pred_sum = pred_sum + gp_recv[step].astype(f32)
    grad_pred_ref[...] = pred_sum
    stores[1].start()

    each(owners, lambda step: send_back(step).wait())
    grad_enc_ref[...] = jnp.dot(
        pick_t, returned[...].reshape(slots, width), preferred_element_type=f32
    ).astype(bf16)
    stores[2].start()

    if reduce_here:
        whole_sum = owner_sum[0, inner].astype(f32)
        for near in ahead:
            for side in range(near == 0, 2):
                owner_copy(near, side).wait()
                whole_sum = whole_sum + owner_recv[near, side].astype(f32)
        grad_w_ref[...] = whole_sum
        stores[3].start()
    for store in stores:
        store.wait()


def finish_kernel(*refs):
    *ends, load_sem, store_sem = refs
    count = len(ends) // 3
    sources, results, held = ends[:count], ends[count : 2 * count], ends[2 * count :]
    loads = [
        pltpu.make_async_copy(sources[slot], held[slot], load_sem.at[slot])
        for slot in range(count)
    ]
    stores = [
        pltpu.make_async_copy(held[slot], results[slot], store_sem.at[slot])
        for slot in range(count)
    ]
    for load in loads:
        load.start()
    for load, store in zip(loads, stores):
        load.wait()
        store.start()
    for store in stores:
        store.wait()


def shards_fn(
    enc_rows,
    dest,
    pred_rows,
    label_ids,
    block_off,
    band_start,
    w_enc,
    w_dec,
    w_out,
    bias_out,
    grad_blank,
    grad_label,
):
    owners = lax.axis_size("dp")
    shards = lax.axis_size("frame")
    rows, width = enc_rows.shape
    kept = grad_blank.shape[1]
    joint = w_enc.shape[1]
    vocab = w_out.shape[1]
    lab_part = pred_rows.shape[0]
    cap = max(TILE_ROWS, 2 * rows // owners)
    per_device = joint // (owners * shards)
    reduce_here = per_device % TILE_ROWS == 0 and owners % 2 == 0
    grad_rows = per_device if reduce_here else joint
    slot_rows = per_device if reduce_here else TILE_ROWS
    outer = owners // 2 if reduce_here else 1
    bf16 = jnp.bfloat16
    hbm = pl.BlockSpec(memory_space=pltpu.HBM)
    exchange = pltpu.VMEM((owners, cap, width), bf16)
    arrays = (
        enc_rows,
        dest[:, 0, :],
        pred_rows,
        label_ids,
        block_off,
        band_start[None, :],
        w_enc,
        w_dec,
        w_out.T,
        bias_out[None, :],
        grad_blank.T,
        grad_label.T,
    )
    fetched = [
        (pltpu.SMEM if slot == 4 else pltpu.VMEM)(array.shape, array.dtype)
        for slot, array in enumerate(arrays)
        if slot != 2
    ]
    outputs = (
        jax.ShapeDtypeStruct((2 * kept, rows), jnp.float32),
        jax.ShapeDtypeStruct((rows, width), bf16),
        jax.ShapeDtypeStruct((lab_part, width), jnp.float32),
        jax.ShapeDtypeStruct((grad_rows, vocab), jnp.float32),
    )
    results = pl.pallas_call(
        functools.partial(joint_kernel, (owners, shards, cap, rows, kept, reduce_here)),
        out_shape=outputs,
        in_specs=[hbm] * len(arrays),
        out_specs=(hbm,) * 4,
        scratch_shapes=[
            exchange,
            exchange,
            exchange,
            exchange,
            pltpu.VMEM((shards, lab_part, width), bf16),
            pltpu.VMEM((outer, 2, shards, slot_rows, vocab), bf16),
            pltpu.VMEM((outer, shards, 2, slot_rows, vocab), bf16),
            pltpu.VMEM((outer, 2, slot_rows, vocab), bf16),
            pltpu.VMEM((outer, 2, slot_rows, vocab), bf16),
            pltpu.VMEM((shards, lab_part, width), bf16),
            pltpu.VMEM((shards, lab_part, width), bf16),
            *fetched,
            pltpu.VMEM(w_out.shape, bf16),
            pltpu.VMEM(w_enc.shape[::-1], bf16),
            pltpu.VMEM(w_dec.shape[::-1], bf16),
            *(pltpu.VMEM(output.shape, output.dtype) for output in outputs),
            pltpu.SemaphoreType.DMA((2, 2, owners)),
            pltpu.SemaphoreType.DMA((2, 2, shards)),
            pltpu.SemaphoreType.DMA((2, outer, shards)),
            pltpu.SemaphoreType.DMA((2, outer, 2)),
            pltpu.SemaphoreType.DMA((len(arrays),)),
            pltpu.SemaphoreType.DMA((len(outputs),)),
        ],
        compiler_params=pltpu.CompilerParams(
            collective_id=0, has_side_effects=True, vmem_limit_bytes=VMEM_BYTES
        ),
    )(*arrays)
    tail = ()
    if not reduce_here:
        *results, grad_w = results
        tail = (lax.psum_scatter(grad_w, ("dp", "frame"), scatter_dimension=0, tiled=True),)
    logp, *others = pl.pallas_call(
        finish_kernel,
        out_shape=tuple(jax.ShapeDtypeStruct(array.shape, array.dtype) for array in results),
        in_specs=[hbm] * len(results),
        out_specs=(hbm,) * len(results),
        scratch_shapes=[
            *(pltpu.VMEM(array.shape, array.dtype) for array in results),
            pltpu.SemaphoreType.DMA((len(results),)),
            pltpu.SemaphoreType.DMA((len(results),)),
        ],
        compiler_params=pltpu.CompilerParams(vmem_limit_bytes=VMEM_BYTES),
    )(*results)
    return (logp.T, *others, *tail)


def solution(mesh):
    rows = P(("dp", "frame"), None)
    return jax.shard_map(
        shards_fn,
        mesh=mesh,
        in_specs=(
            rows,
            P(None, "frame", None),
            rows,
            P("dp", None),
            P(("dp", "frame")),
            P(("dp", "frame")),
            P(),
            P(),
            P(),
            P(),
            rows,
            rows,
        ),
        out_specs=(rows, rows, rows, rows),
        check_vma=False,
    )
```

```python
import functools

import jax
import jax.numpy as jnp
from jax import lax
from jax.experimental import pallas as pl
from jax.experimental.pallas import tpu as pltpu
from jax.sharding import PartitionSpec as P

BLOCK = 64
TILE_ROWS = 16
VMEM_BYTES = 64 * 1024 * 1024
MESH = pl.DeviceIdType.MESH


def log2(size):
    assert size & (size - 1) == 0
    return size.bit_length() - 1


def joint_kernel(
    dims,
    enc_hbm,
    dest_hbm,
    pred_ref,
    label_hbm,
    off_hbm,
    band_hbm,
    w_enc_hbm,
    w_dec_hbm,
    w_out_hbm,
    bias_hbm,
    blank_hbm,
    cot_hbm,
    logp_hbm,
    grad_enc_hbm,
    grad_pred_hbm,
    grad_w_hbm,
    outbound,
    arrived,
    outgoing,
    returned,
    pred_all,
    piece_send,
    piece_recv,
    owner_sum,
    pair_recv,
    pair_sum,
    owner_recv,
    gp_send,
    gp_recv,
    enc_ref,
    dest_ref,
    label_ref,
    off_ref,
    band_ref,
    w_enc_ref,
    w_dec_ref,
    w_out_ref,
    bias_ref,
    blank_ref,
    cot_ref,
    w_out_t,
    w_enc_t,
    w_dec_t,
    logp_ref,
    grad_enc_ref,
    grad_pred_ref,
    grad_w_ref,
    dp_sem,
    frame_sem,
    piece_sem,
    owner_sem,
    load_sem,
    store_sem,
):
    owners, shards, cap, rows, kept, reduce_here = dims
    me = lax.axis_index("dp")
    part = lax.axis_index("frame")
    width = enc_hbm.shape[1]
    vocab = w_out_hbm.shape[0]
    lab_part = pred_ref.shape[0]
    labels = shards * lab_part
    slots = owners * cap
    f32, bf16 = jnp.float32, jnp.bfloat16

    def iota(shape, dim):
        return lax.broadcasted_iota(jnp.int32, shape, dim)

    def to_owner(step, src, dst, kind):
        peer = lax.rem(me + step, owners)
        return pltpu.make_async_remote_copy(
            src_ref=src(peer),
            dst_ref=dst(step),
            send_sem=dp_sem.at[kind, 0, step],
            recv_sem=dp_sem.at[kind, 1, step],
            device_id={"dp": peer},
            device_id_type=MESH,
        )

    def to_shard(step, src, dst, kind):
        peer = lax.rem(part + step, shards)
        return pltpu.make_async_remote_copy(
            src_ref=src(peer),
            dst_ref=dst(step),
            send_sem=frame_sem.at[kind, 0, step],
            recv_sem=frame_sem.at[kind, 1, step],
            device_id={"frame": peer},
            device_id_type=MESH,
        )

    def each(count, act):
        if count <= 8:
            for step in sorted(range(1, count), key=lambda step: abs(2 * step - count)):
                act(step)
        else:

            def body(step, carry):
                act(step)
                return carry

            lax.fori_loop(1, count, body, 0)

    stores = [
        pltpu.make_async_copy(src, dst, store_sem.at[slot])
        for slot, (src, dst) in enumerate(
            [
                (logp_ref, logp_hbm),
                (grad_pred_ref, grad_pred_hbm),
                (grad_enc_ref, grad_enc_hbm),
                (grad_w_ref, grad_w_hbm),
            ]
        )
    ]

    barrier = pltpu.get_barrier_semaphore()

    def greet_owner(step):
        pl.semaphore_signal(
            barrier, inc=1, device_id={"dp": lax.rem(me + step, owners)}, device_id_type=MESH
        )

    def greet_shard(step):
        pl.semaphore_signal(
            barrier, inc=1, device_id={"frame": lax.rem(part + step, shards)}, device_id_type=MESH
        )

    each(owners, greet_owner)
    each(shards, greet_shard)

    pairs = [
        (dest_hbm, dest_ref),
        (enc_hbm, enc_ref),
        (off_hbm, off_ref),
        (band_hbm, band_ref),
        (blank_hbm, blank_ref),
        (cot_hbm, cot_ref),
        (label_hbm, label_ref),
        (pred_ref, pred_all.at[part]),
        (w_dec_hbm, w_dec_ref),
        (w_enc_hbm, w_enc_ref),
        (w_out_hbm, w_out_ref),
        (bias_hbm, bias_ref),
    ]
    loads = [
        pltpu.make_async_copy(src, dst, load_sem.at[slot]) for slot, (src, dst) in enumerate(pairs)
    ]
    for load in loads:
        load.start()
    loads[0].wait()

    shape = (slots, rows)
    slot_owner = lax.shift_right_logical(iota(shape, 0), log2(cap))
    slot_rank = iota(shape, 0) & (cap - 1)
    lane = iota(shape, 1)
    my_dest = dest_ref[pl.ds(me, 1), :]

    def count(source, sums):
        out_sum, in_sum = sums
        owner_of = lax.shift_right_logical(dest_ref[pl.ds(source, 1), :], log2(rows))
        before_me = (source < me).astype(f32)
        out_sum = out_sum + jnp.where(owner_of == slot_owner, before_me, 0.0)
        mine = jnp.where(owner_of == me, 1.0, 0.0)
        in_sum = in_sum + jnp.where(slot_owner > source, mine, 0.0)
        return out_sum, in_sum

    sums = (jnp.zeros(shape, f32), jnp.zeros(shape, f32))
    if owners <= 8:
        for source in range(owners):
            sums = count(source, sums)
    else:
        sums = lax.fori_loop(0, owners, count, sums)
    out_row = jnp.sum(sums[0], axis=1, keepdims=True).astype(jnp.int32) + slot_rank
    in_row = jnp.sum(sums[1], axis=1, keepdims=True).astype(jnp.int32) + slot_rank
    pick = (my_dest == slot_owner * rows + out_row) & (out_row < rows)
    pick = jnp.where(pick, 1.0, 0.0)
    place = jnp.where(lane == in_row, 1.0, 0.0)
    loads[1].wait()
    out_rows = jnp.dot(pick.astype(bf16), enc_ref[...], preferred_element_type=f32).astype(bf16)
    outbound[...] = out_rows.reshape(owners, cap, width)

    pl.semaphore_wait(barrier, owners - 1 + shards - 1)

    send_enc = functools.partial(
        to_owner, src=lambda peer: outbound.at[peer], dst=lambda step: arrived.at[me], kind=0
    )
    send_pred = functools.partial(
        to_shard, src=lambda peer: pred_ref, dst=lambda step: pred_all.at[part], kind=0
    )
    each(owners, lambda step: send_enc(step).start())
    each(shards, lambda step: send_pred(step).start())
    arrived[me] = outbound[me]
    for load in loads[2:8]:
        load.wait()

    half = iota((1, rows), 1) // BLOCK
    base_row = band_ref[...]
    for block in range(rows // BLOCK):
        base_row = base_row + jnp.where(half == block, off_ref[block], 0)
    cols = jnp.concatenate(
        [
            base_row.astype(f32),
            jnp.zeros((1, rows), f32),
            blank_ref[...],
            cot_ref[...],
        ],
        axis=0,
    ).T
    base_col = cols[:, 0:1].astype(jnp.int32)
    gather_hot = jnp.concatenate(
        [
            jnp.where(iota((rows, labels), 1) == base_col + k, 1.0, 0.0)
            for k in range(kept)
        ],
        axis=0,
    )
    scatter_hot = jnp.concatenate(
        [
            jnp.where(iota((labels, rows), 0) == base_row + k, 1.0, 0.0)
            for k in range(kept)
        ],
        axis=1,
    ).astype(bf16)
    emitted = jnp.sum(gather_hot * label_ref[...].astype(f32), axis=1, keepdims=True)
    emitted = emitted.astype(jnp.int32)
    place_t = place.T.astype(bf16)
    pick_t = pick.T.astype(bf16)
    place = place.astype(bf16)

    each(shards, lambda step: send_pred(step).wait())
    loads[8].wait()
    dec_joint = jnp.dot(
        pred_all[...].reshape(labels, width), w_dec_ref[...], preferred_element_type=f32
    ).astype(bf16)
    dec_rows = jnp.dot(gather_hot.astype(bf16), dec_joint, preferred_element_type=f32)

    for load in loads[9:]:
        load.wait()
    w_out_t[...] = w_out_ref[...].T
    w_enc_t[...] = w_enc_ref[...].T
    w_dec_t[...] = w_dec_ref[...].T
    each(owners, lambda step: send_enc(step).wait())
    enc_owned = jnp.dot(
        place_t, arrived[...].reshape(slots, width), preferred_element_type=f32
    ).astype(bf16)
    enc_joint = jnp.dot(enc_owned, w_enc_ref[...], preferred_element_type=f32)
    word = iota((rows, vocab), 1)
    hiddens, hiddens_t, dlogits, blank_logps, label_logps = [], [], [], [], []
    for k in range(kept):
        span = slice(k * rows, (k + 1) * rows)
        hidden = jnp.tanh(enc_joint + dec_rows[span]).astype(bf16)
        logits = jnp.dot(hidden, w_out_t[...], preferred_element_type=f32) + bias_ref[...]
        hiddens.append(hidden)
        hiddens_t.append(hidden.T)
        shifted = logits - jnp.max(logits, axis=1, keepdims=True)
        powers = jnp.exp(shifted)
        total = jnp.sum(powers, axis=1, keepdims=True)
        log_total = jnp.log(total)
        is_label = word == emitted[span]
        blank_logps.append(shifted[:, 0:1] - log_total)
        label_logps.append(
            jnp.sum(jnp.where(is_label, shifted, 0.0), axis=1, keepdims=True) - log_total
        )
        cot_blank = cols[:, 2 + k : 3 + k]
        cot_label = cols[:, 2 + kept + k : 3 + kept + k]
        scale = (cot_blank + cot_label) / total
        dlogits.append(
            (
                jnp.where(word == 0, cot_blank, 0.0)
                + jnp.where(is_label, cot_label, 0.0)
                - powers * scale
            ).astype(bf16)
        )

    grad_w = jnp.dot(
        jnp.concatenate(hiddens_t, axis=1),
        jnp.concatenate(dlogits, axis=0),
        preferred_element_type=f32,
    ).astype(bf16)
    inner, outer_at, outer = lax.rem(me, 2), me // 2, owners // 2
    ahead = sorted(range(outer), key=lambda step: (step == 0, abs(2 * step - outer)))

    def piece_copy(near, step):
        peer = lax.rem(part + step, shards)
        return pltpu.make_async_remote_copy(
            src_ref=piece_send.at[lax.rem(outer_at + near, outer), :, peer],
            dst_ref=piece_recv.at[near, step],
            send_sem=piece_sem.at[0, near, step],
            recv_sem=piece_sem.at[1, near, step],
            device_id={"frame": peer},
            device_id_type=MESH,
        )

    def pair_copy(near):
        return pltpu.make_async_remote_copy(
            src_ref=owner_sum.at[near, 1 - inner],
            dst_ref=pair_recv.at[near],
            send_sem=owner_sem.at[0, near, 0],
            recv_sem=owner_sem.at[1, near, 0],
            device_id={"dp": me + 1 - 2 * inner},
            device_id_type=MESH,
        )

    def owner_copy(near):
        return pltpu.make_async_remote_copy(
            src_ref=pair_sum.at[near],
            dst_ref=owner_recv.at[near],
            send_sem=owner_sem.at[0, near, 1],
            recv_sem=owner_sem.at[1, near, 1],
            device_id={"dp": 2 * lax.rem(outer_at + near, outer) + inner},
            device_id_type=MESH,
        )

    def sum_piece(near):
        for step in range(1, shards):
            piece_copy(near, step).wait()
        piece = piece_send[lax.rem(outer_at + near, outer), :, part].astype(f32)
        for step in range(1, shards):
            piece = piece + piece_recv[near, step].astype(f32)
        owner_sum[near] = piece.astype(bf16)
        pair_copy(near).start()

    def sum_pair(near):
        pair_copy(near).wait()
        pair = owner_sum[near, inner].astype(f32) + pair_recv[near].astype(f32)
        pair_sum[near] = pair.astype(bf16)
        if near:
            owner_copy(near).start()

    if reduce_here:
        piece_send[...] = grad_w.reshape(piece_send.shape)
        for near in ahead:
            for step in range(1, shards):
                piece_copy(near, step).start()
    else:
        grad_w_ref[...] = grad_w.astype(f32)
        stores[3].start()

    dzs = []
    for k in range(kept):
        back = jnp.dot(dlogits[k], w_out_ref[...], preferred_element_type=f32)
        hidden_f = hiddens[k].astype(f32)
        dzs.append(back * (1.0 - hidden_f * hidden_f))
    enc_grad = dzs[0]
    for dz in dzs[1:]:
        enc_grad = enc_grad + dz
    owned_grad = lax.dot_general(
        enc_grad.astype(bf16), w_enc_t[...], (((1,), (0,)), ((), ())), preferred_element_type=f32
    ).astype(bf16)
    outgoing[...] = (
        jnp.dot(place, owned_grad, preferred_element_type=f32)
        .astype(bf16)
        .reshape(owners, cap, width)
    )
    send_back = functools.partial(
        to_owner, src=lambda peer: outgoing.at[peer], dst=lambda step: returned.at[me], kind=1
    )
    each(owners, lambda step: send_back(step).start())
    returned[me] = outgoing[me]

    if reduce_here:
        for at, near in enumerate(ahead[:2]):
            sum_piece(near)
            if at:
                sum_pair(ahead[at - 1])

    dz_rows = jnp.concatenate([dz.astype(bf16) for dz in dzs], axis=0)
    dec_grad = jnp.dot(scatter_hot, dz_rows, preferred_element_type=f32)
    gp_send[...] = (
        lax.dot_general(
            dec_grad.astype(bf16),
            w_dec_t[...],
            (((1,), (0,)), ((), ())),
            preferred_element_type=f32,
        )
        .astype(bf16)
        .reshape(shards, lab_part, width)
    )
    send_gp = functools.partial(
        to_shard, src=lambda peer: gp_send.at[peer], dst=lambda step: gp_recv.at[step], kind=1
    )
    each(shards, lambda step: send_gp(step).start())

    if reduce_here:
        for at, near in enumerate(ahead[2:], 2):
            sum_piece(near)
            sum_pair(ahead[at - 1])
        sum_pair(ahead[-1])

    logp_cols = jnp.concatenate(
        blank_logps + label_logps + [jnp.zeros((rows, 8 - 2 * kept), f32)], axis=1
    )
    logp_ref[...] = logp_cols.T[: 2 * kept]
    stores[0].start()

    each(shards, lambda step: send_gp(step).wait())
    pred_sum = gp_send[part].astype(f32)
    for step in range(1, shards):
        pred_sum = pred_sum + gp_recv[step].astype(f32)
    grad_pred_ref[...] = pred_sum
    stores[1].start()

    each(owners, lambda step: send_back(step).wait())
    grad_enc_ref[...] = jnp.dot(
        pick_t, returned[...].reshape(slots, width), preferred_element_type=f32
    ).astype(bf16)
    stores[2].start()

    if reduce_here:
        whole_sum = pair_sum[0].astype(f32)
        for near in ahead[:-1]:
            owner_copy(near).wait()
            whole_sum = whole_sum + owner_recv[near].astype(f32)
        grad_w_ref[...] = whole_sum
        stores[3].start()
    for store in stores:
        store.wait()


def finish_kernel(*refs):
    *ends, load_sem, store_sem = refs
    count = len(ends) // 3
    sources, results, held = ends[:count], ends[count : 2 * count], ends[2 * count :]
    loads = [
        pltpu.make_async_copy(sources[slot], held[slot], load_sem.at[slot])
        for slot in range(count)
    ]
    stores = [
        pltpu.make_async_copy(held[slot], results[slot], store_sem.at[slot])
        for slot in range(count)
    ]
    for load in loads:
        load.start()
    for load, store in zip(loads, stores):
        load.wait()
        store.start()
    for store in stores:
        store.wait()


def shards_fn(
    enc_rows,
    dest,
    pred_rows,
    label_ids,
    block_off,
    band_start,
    w_enc,
    w_dec,
    w_out,
    bias_out,
    grad_blank,
    grad_label,
):
    owners = lax.axis_size("dp")
    shards = lax.axis_size("frame")
    rows, width = enc_rows.shape
    kept = grad_blank.shape[1]
    joint = w_enc.shape[1]
    vocab = w_out.shape[1]
    lab_part = pred_rows.shape[0]
    cap = max(TILE_ROWS, 2 * rows // owners)
    per_device = joint // (owners * shards)
    reduce_here = per_device % TILE_ROWS == 0 and owners % 2 == 0
    grad_rows = per_device if reduce_here else joint
    slot_rows = per_device if reduce_here else TILE_ROWS
    outer = owners // 2 if reduce_here else 1
    bf16 = jnp.bfloat16
    hbm = pl.BlockSpec(memory_space=pltpu.HBM)
    exchange = pltpu.VMEM((owners, cap, width), bf16)
    arrays = (
        enc_rows,
        dest[:, 0, :],
        pred_rows,
        label_ids,
        block_off,
        band_start[None, :],
        w_enc,
        w_dec,
        w_out.T,
        bias_out[None, :],
        grad_blank.T,
        grad_label.T,
    )
    fetched = [
        (pltpu.SMEM if slot == 4 else pltpu.VMEM)(array.shape, array.dtype)
        for slot, array in enumerate(arrays)
        if slot != 2
    ]
    outputs = (
        jax.ShapeDtypeStruct((2 * kept, rows), jnp.float32),
        jax.ShapeDtypeStruct((rows, width), bf16),
        jax.ShapeDtypeStruct((lab_part, width), jnp.float32),
        jax.ShapeDtypeStruct((grad_rows, vocab), jnp.float32),
    )
    results = pl.pallas_call(
        functools.partial(joint_kernel, (owners, shards, cap, rows, kept, reduce_here)),
        out_shape=outputs,
        in_specs=[hbm] * len(arrays),
        out_specs=(hbm,) * 4,
        scratch_shapes=[
            exchange,
            exchange,
            exchange,
            exchange,
            pltpu.VMEM((shards, lab_part, width), bf16),
            pltpu.VMEM((outer, 2, shards, slot_rows, vocab), bf16),
            pltpu.VMEM((outer, shards, 2, slot_rows, vocab), bf16),
            pltpu.VMEM((outer, 2, slot_rows, vocab), bf16),
            pltpu.VMEM((outer, slot_rows, vocab), bf16),
            pltpu.VMEM((outer, slot_rows, vocab), bf16),
            pltpu.VMEM((outer, slot_rows, vocab), bf16),
            pltpu.VMEM((shards, lab_part, width), bf16),
            pltpu.VMEM((shards, lab_part, width), bf16),
            *fetched,
            pltpu.VMEM(w_out.shape, bf16),
            pltpu.VMEM(w_enc.shape[::-1], bf16),
            pltpu.VMEM(w_dec.shape[::-1], bf16),
            *(pltpu.VMEM(output.shape, output.dtype) for output in outputs),
            pltpu.SemaphoreType.DMA((2, 2, owners)),
            pltpu.SemaphoreType.DMA((2, 2, shards)),
            pltpu.SemaphoreType.DMA((2, outer, shards)),
            pltpu.SemaphoreType.DMA((2, outer, 2)),
            pltpu.SemaphoreType.DMA((len(arrays),)),
            pltpu.SemaphoreType.DMA((len(outputs),)),
        ],
        compiler_params=pltpu.CompilerParams(
            collective_id=0, has_side_effects=True, vmem_limit_bytes=VMEM_BYTES
        ),
    )(*arrays)
    tail = ()
    if not reduce_here:
        *results, grad_w = results
        tail = (lax.psum_scatter(grad_w, ("dp", "frame"), scatter_dimension=0, tiled=True),)
    logp, *others = pl.pallas_call(
        finish_kernel,
        out_shape=tuple(jax.ShapeDtypeStruct(array.shape, array.dtype) for array in results),
        in_specs=[hbm] * len(results),
        out_specs=(hbm,) * len(results),
        scratch_shapes=[
            *(pltpu.VMEM(array.shape, array.dtype) for array in results),
            pltpu.SemaphoreType.DMA((len(results),)),
            pltpu.SemaphoreType.DMA((len(results),)),
        ],
        compiler_params=pltpu.CompilerParams(vmem_limit_bytes=VMEM_BYTES),
    )(*results)
    return (logp.T, *others, *tail)


def solution(mesh):
    rows = P(("dp", "frame"), None)
    return jax.shard_map(
        shards_fn,
        mesh=mesh,
        in_specs=(
            rows,
            P(None, "frame", None),
            rows,
            P("dp", None),
            P(("dp", "frame")),
            P(("dp", "frame")),
            P(),
            P(),
            P(),
            P(),
            rows,
            rows,
        ),
        out_specs=(rows, rows, rows, rows),
        check_vma=False,
    )
```

```python
import functools

import jax
import jax.numpy as jnp
from jax import lax
from jax.experimental import pallas as pl
from jax.experimental.pallas import tpu as pltpu
from jax.sharding import PartitionSpec as P

BLOCK = 64
TILE_ROWS = 16
VMEM_BYTES = 64 * 1024 * 1024
MESH = pl.DeviceIdType.MESH


def log2(size):
    assert size & (size - 1) == 0
    return size.bit_length() - 1


def joint_kernel(
    dims,
    enc_hbm,
    dest_hbm,
    pred_ref,
    label_hbm,
    off_hbm,
    band_hbm,
    w_enc_hbm,
    w_dec_hbm,
    w_out_hbm,
    bias_hbm,
    blank_hbm,
    cot_hbm,
    logp_hbm,
    grad_enc_hbm,
    grad_pred_hbm,
    grad_w_hbm,
    outbound,
    arrived,
    outgoing,
    returned,
    pred_all,
    piece_send,
    core_recv,
    core_sum,
    piece_recv,
    owner_sum,
    owner_recv,
    gp_send,
    gp_recv,
    enc_ref,
    dest_ref,
    label_ref,
    off_ref,
    band_ref,
    w_enc_ref,
    w_dec_ref,
    w_out_ref,
    bias_ref,
    blank_ref,
    cot_ref,
    w_out_t,
    w_enc_t,
    w_dec_t,
    logp_ref,
    grad_enc_ref,
    grad_pred_ref,
    grad_w_ref,
    dp_sem,
    frame_sem,
    piece_sem,
    owner_sem,
    load_sem,
    store_sem,
):
    owners, shards, cap, rows, kept, reduce_here = dims
    me = lax.axis_index("dp")
    part = lax.axis_index("frame")
    width = enc_hbm.shape[1]
    vocab = w_out_hbm.shape[0]
    lab_part = pred_ref.shape[0]
    labels = shards * lab_part
    slots = owners * cap
    f32, bf16 = jnp.float32, jnp.bfloat16

    def iota(shape, dim):
        return lax.broadcasted_iota(jnp.int32, shape, dim)

    def to_owner(step, src, dst, kind):
        peer = lax.rem(me + step, owners)
        return pltpu.make_async_remote_copy(
            src_ref=src(peer),
            dst_ref=dst(step),
            send_sem=dp_sem.at[kind, 0, step],
            recv_sem=dp_sem.at[kind, 1, step],
            device_id={"dp": peer},
            device_id_type=MESH,
        )

    def to_shard(step, src, dst, kind):
        peer = lax.rem(part + step, shards)
        return pltpu.make_async_remote_copy(
            src_ref=src(peer),
            dst_ref=dst(step),
            send_sem=frame_sem.at[kind, 0, step],
            recv_sem=frame_sem.at[kind, 1, step],
            device_id={"frame": peer},
            device_id_type=MESH,
        )

    def each(count, act):
        if count <= 8:
            for step in sorted(range(1, count), key=lambda step: abs(2 * step - count)):
                act(step)
        else:

            def body(step, carry):
                act(step)
                return carry

            lax.fori_loop(1, count, body, 0)

    stores = [
        pltpu.make_async_copy(src, dst, store_sem.at[slot])
        for slot, (src, dst) in enumerate(
            [
                (logp_ref, logp_hbm),
                (grad_pred_ref, grad_pred_hbm),
                (grad_enc_ref, grad_enc_hbm),
                (grad_w_ref, grad_w_hbm),
            ]
        )
    ]

    barrier = pltpu.get_barrier_semaphore()

    def greet_owner(step):
        pl.semaphore_signal(
            barrier, inc=1, device_id={"dp": lax.rem(me + step, owners)}, device_id_type=MESH
        )

    def greet_shard(step):
        pl.semaphore_signal(
            barrier, inc=1, device_id={"frame": lax.rem(part + step, shards)}, device_id_type=MESH
        )

    each(owners, greet_owner)
    each(shards, greet_shard)

    pairs = [
        (dest_hbm, dest_ref),
        (enc_hbm, enc_ref),
        (off_hbm, off_ref),
        (band_hbm, band_ref),
        (blank_hbm, blank_ref),
        (cot_hbm, cot_ref),
        (label_hbm, label_ref),
        (pred_ref, pred_all.at[part]),
        (w_dec_hbm, w_dec_ref),
        (w_enc_hbm, w_enc_ref),
        (w_out_hbm, w_out_ref),
        (bias_hbm, bias_ref),
    ]
    loads = [
        pltpu.make_async_copy(src, dst, load_sem.at[slot]) for slot, (src, dst) in enumerate(pairs)
    ]
    for load in loads:
        load.start()
    loads[0].wait()

    shape = (slots, rows)
    slot_owner = lax.shift_right_logical(iota(shape, 0), log2(cap))
    slot_rank = iota(shape, 0) & (cap - 1)
    lane = iota(shape, 1)
    my_dest = dest_ref[pl.ds(me, 1), :]

    def count(source, sums):
        out_sum, in_sum = sums
        owner_of = lax.shift_right_logical(dest_ref[pl.ds(source, 1), :], log2(rows))
        before_me = (source < me).astype(f32)
        out_sum = out_sum + jnp.where(owner_of == slot_owner, before_me, 0.0)
        mine = jnp.where(owner_of == me, 1.0, 0.0)
        in_sum = in_sum + jnp.where(slot_owner > source, mine, 0.0)
        return out_sum, in_sum

    sums = (jnp.zeros(shape, f32), jnp.zeros(shape, f32))
    if owners <= 8:
        for source in range(owners):
            sums = count(source, sums)
    else:
        sums = lax.fori_loop(0, owners, count, sums)
    out_row = jnp.sum(sums[0], axis=1, keepdims=True).astype(jnp.int32) + slot_rank
    in_row = jnp.sum(sums[1], axis=1, keepdims=True).astype(jnp.int32) + slot_rank
    pick = (my_dest == slot_owner * rows + out_row) & (out_row < rows)
    pick = jnp.where(pick, 1.0, 0.0)
    place = jnp.where(lane == in_row, 1.0, 0.0)
    loads[1].wait()
    out_rows = jnp.dot(pick.astype(bf16), enc_ref[...], preferred_element_type=f32).astype(bf16)
    outbound[...] = out_rows.reshape(owners, cap, width)

    pl.semaphore_wait(barrier, owners - 1 + shards - 1)

    send_enc = functools.partial(
        to_owner, src=lambda peer: outbound.at[peer], dst=lambda step: arrived.at[me], kind=0
    )
    send_pred = functools.partial(
        to_shard, src=lambda peer: pred_ref, dst=lambda step: pred_all.at[part], kind=0
    )
    each(owners, lambda step: send_enc(step).start())
    each(shards, lambda step: send_pred(step).start())
    arrived[me] = outbound[me]
    for load in loads[2:8]:
        load.wait()

    half = iota((1, rows), 1) // BLOCK
    base_row = band_ref[...]
    for block in range(rows // BLOCK):
        base_row = base_row + jnp.where(half == block, off_ref[block], 0)
    cols = jnp.concatenate(
        [
            base_row.astype(f32),
            jnp.zeros((1, rows), f32),
            blank_ref[...],
            cot_ref[...],
        ],
        axis=0,
    ).T
    base_col = cols[:, 0:1].astype(jnp.int32)
    gather_hot = jnp.concatenate(
        [
            jnp.where(iota((rows, labels), 1) == base_col + k, 1.0, 0.0)
            for k in range(kept)
        ],
        axis=0,
    )
    scatter_hot = jnp.concatenate(
        [
            jnp.where(iota((labels, rows), 0) == base_row + k, 1.0, 0.0)
            for k in range(kept)
        ],
        axis=1,
    ).astype(bf16)
    emitted = jnp.sum(gather_hot * label_ref[...].astype(f32), axis=1, keepdims=True)
    emitted = emitted.astype(jnp.int32)
    place_t = place.T.astype(bf16)
    pick_t = pick.T.astype(bf16)
    place = place.astype(bf16)

    each(shards, lambda step: send_pred(step).wait())
    loads[8].wait()
    dec_joint = jnp.dot(
        pred_all[...].reshape(labels, width), w_dec_ref[...], preferred_element_type=f32
    ).astype(bf16)
    dec_rows = jnp.dot(gather_hot.astype(bf16), dec_joint, preferred_element_type=f32)

    for load in loads[9:]:
        load.wait()
    w_out_t[...] = w_out_ref[...].T
    w_enc_t[...] = w_enc_ref[...].T
    w_dec_t[...] = w_dec_ref[...].T
    each(owners, lambda step: send_enc(step).wait())
    enc_owned = jnp.dot(
        place_t, arrived[...].reshape(slots, width), preferred_element_type=f32
    ).astype(bf16)
    enc_joint = jnp.dot(enc_owned, w_enc_ref[...], preferred_element_type=f32)
    word = iota((rows, vocab), 1)
    hiddens, hiddens_t, dlogits, blank_logps, label_logps = [], [], [], [], []
    for k in range(kept):
        span = slice(k * rows, (k + 1) * rows)
        hidden = jnp.tanh(enc_joint + dec_rows[span]).astype(bf16)
        logits = jnp.dot(hidden, w_out_t[...], preferred_element_type=f32) + bias_ref[...]
        hiddens.append(hidden)
        hiddens_t.append(hidden.T)
        shifted = logits - jnp.max(logits, axis=1, keepdims=True)
        powers = jnp.exp(shifted)
        total = jnp.sum(powers, axis=1, keepdims=True)
        log_total = jnp.log(total)
        is_label = word == emitted[span]
        blank_logps.append(shifted[:, 0:1] - log_total)
        label_logps.append(
            jnp.sum(jnp.where(is_label, shifted, 0.0), axis=1, keepdims=True) - log_total
        )
        cot_blank = cols[:, 2 + k : 3 + k]
        cot_label = cols[:, 2 + kept + k : 3 + kept + k]
        scale = (cot_blank + cot_label) / total
        dlogits.append(
            (
                jnp.where(word == 0, cot_blank, 0.0)
                + jnp.where(is_label, cot_label, 0.0)
                - powers * scale
            ).astype(bf16)
        )

    grad_w = jnp.dot(
        jnp.concatenate(hiddens_t, axis=1),
        jnp.concatenate(dlogits, axis=0),
        preferred_element_type=f32,
    ).astype(bf16)
    inner, outer_at, outer = lax.rem(me, 2), me // 2, owners // 2
    ahead = sorted(range(outer), key=lambda step: (step == 0, abs(2 * step - outer)))

    core, y = lax.rem(part, 2), part // 2

    def core_copy(near):
        return pltpu.make_async_remote_copy(
            src_ref=piece_send.at[lax.rem(outer_at + near, outer), :, :, 1 - core],
            dst_ref=core_recv.at[near],
            send_sem=piece_sem.at[0, near, 0],
            recv_sem=piece_sem.at[1, near, 0],
            device_id={"frame": part + 1 - 2 * core},
            device_id_type=MESH,
        )

    def piece_copy(near):
        return pltpu.make_async_remote_copy(
            src_ref=core_sum.at[near, :, 1 - y],
            dst_ref=piece_recv.at[near],
            send_sem=piece_sem.at[0, near, 1],
            recv_sem=piece_sem.at[1, near, 1],
            device_id={"frame": lax.rem(part + 2, shards)},
            device_id_type=MESH,
        )

    def owner_copy(near, side):
        to_inner = lax.rem(inner + side, 2)
        return pltpu.make_async_remote_copy(
            src_ref=owner_sum.at[near, to_inner],
            dst_ref=owner_recv.at[near, side],
            send_sem=owner_sem.at[0, near, side],
            recv_sem=owner_sem.at[1, near, side],
            device_id={"dp": 2 * lax.rem(outer_at + near, outer) + to_inner},
            device_id_type=MESH,
        )

    if reduce_here:
        piece_send[...] = grad_w.reshape(piece_send.shape)
        for near in ahead:
            core_copy(near).start()
    else:
        grad_w_ref[...] = grad_w.astype(f32)
        stores[3].start()

    dzs = []
    for k in range(kept):
        back = jnp.dot(dlogits[k], w_out_ref[...], preferred_element_type=f32)
        hidden_f = hiddens[k].astype(f32)
        dzs.append(back * (1.0 - hidden_f * hidden_f))
    enc_grad = dzs[0]
    for dz in dzs[1:]:
        enc_grad = enc_grad + dz
    owned_grad = lax.dot_general(
        enc_grad.astype(bf16), w_enc_t[...], (((1,), (0,)), ((), ())), preferred_element_type=f32
    ).astype(bf16)
    outgoing[...] = (
        jnp.dot(place, owned_grad, preferred_element_type=f32)
        .astype(bf16)
        .reshape(owners, cap, width)
    )
    send_back = functools.partial(
        to_owner, src=lambda peer: outgoing.at[peer], dst=lambda step: returned.at[me], kind=1
    )
    each(owners, lambda step: send_back(step).start())
    returned[me] = outgoing[me]

    if reduce_here:
        for near in ahead:
            core_copy(near).wait()
            own = piece_send[lax.rem(outer_at + near, outer), :, :, core].astype(f32)
            core_sum[near] = (own + core_recv[near].astype(f32)).astype(bf16)
            piece_copy(near).start()

    dz_rows = jnp.concatenate([dz.astype(bf16) for dz in dzs], axis=0)
    dec_grad = jnp.dot(scatter_hot, dz_rows, preferred_element_type=f32)
    gp_send[...] = (
        lax.dot_general(
            dec_grad.astype(bf16),
            w_dec_t[...],
            (((1,), (0,)), ((), ())),
            preferred_element_type=f32,
        )
        .astype(bf16)
        .reshape(shards, lab_part, width)
    )
    send_gp = functools.partial(
        to_shard, src=lambda peer: gp_send.at[peer], dst=lambda step: gp_recv.at[step], kind=1
    )
    each(shards, lambda step: send_gp(step).start())

    if reduce_here:
        for near in ahead:
            piece_copy(near).wait()
            piece = core_sum[near, :, y].astype(f32) + piece_recv[near].astype(f32)
            owner_sum[near] = piece.astype(bf16)
            for side in range(near == 0, 2):
                owner_copy(near, side).start()

    logp_cols = jnp.concatenate(
        blank_logps + label_logps + [jnp.zeros((rows, 8 - 2 * kept), f32)], axis=1
    )
    logp_ref[...] = logp_cols.T[: 2 * kept]
    stores[0].start()

    each(shards, lambda step: send_gp(step).wait())
    pred_sum = gp_send[part].astype(f32)
    for step in range(1, shards):
        pred_sum = pred_sum + gp_recv[step].astype(f32)
    grad_pred_ref[...] = pred_sum
    stores[1].start()

    each(owners, lambda step: send_back(step).wait())
    grad_enc_ref[...] = jnp.dot(
        pick_t, returned[...].reshape(slots, width), preferred_element_type=f32
    ).astype(bf16)
    stores[2].start()

    if reduce_here:
        whole_sum = owner_sum[0, inner].astype(f32)
        for near in ahead:
            for side in range(near == 0, 2):
                owner_copy(near, side).wait()
                whole_sum = whole_sum + owner_recv[near, side].astype(f32)
        grad_w_ref[...] = whole_sum
        stores[3].start()
    for store in stores:
        store.wait()


def finish_kernel(*refs):
    *ends, load_sem, store_sem = refs
    count = len(ends) // 3
    sources, results, held = ends[:count], ends[count : 2 * count], ends[2 * count :]
    loads = [
        pltpu.make_async_copy(sources[slot], held[slot], load_sem.at[slot])
        for slot in range(count)
    ]
    stores = [
        pltpu.make_async_copy(held[slot], results[slot], store_sem.at[slot])
        for slot in range(count)
    ]
    for load in loads:
        load.start()
    for load, store in zip(loads, stores):
        load.wait()
        store.start()
    for store in stores:
        store.wait()


def shards_fn(
    enc_rows,
    dest,
    pred_rows,
    label_ids,
    block_off,
    band_start,
    w_enc,
    w_dec,
    w_out,
    bias_out,
    grad_blank,
    grad_label,
):
    owners = lax.axis_size("dp")
    shards = lax.axis_size("frame")
    rows, width = enc_rows.shape
    kept = grad_blank.shape[1]
    joint = w_enc.shape[1]
    vocab = w_out.shape[1]
    lab_part = pred_rows.shape[0]
    cap = max(TILE_ROWS, 2 * rows // owners)
    per_device = joint // (owners * shards)
    reduce_here = per_device % TILE_ROWS == 0 and owners % 2 == 0 and shards == 4
    grad_rows = per_device if reduce_here else joint
    slot_rows = per_device if reduce_here else TILE_ROWS
    outer = owners // 2 if reduce_here else 1
    bf16 = jnp.bfloat16
    hbm = pl.BlockSpec(memory_space=pltpu.HBM)
    exchange = pltpu.VMEM((owners, cap, width), bf16)
    arrays = (
        enc_rows,
        dest[:, 0, :],
        pred_rows,
        label_ids,
        block_off,
        band_start[None, :],
        w_enc,
        w_dec,
        w_out.T,
        bias_out[None, :],
        grad_blank.T,
        grad_label.T,
    )
    fetched = [
        (pltpu.SMEM if slot == 4 else pltpu.VMEM)(array.shape, array.dtype)
        for slot, array in enumerate(arrays)
        if slot != 2
    ]
    outputs = (
        jax.ShapeDtypeStruct((2 * kept, rows), jnp.float32),
        jax.ShapeDtypeStruct((rows, width), bf16),
        jax.ShapeDtypeStruct((lab_part, width), jnp.float32),
        jax.ShapeDtypeStruct((grad_rows, vocab), jnp.float32),
    )
    results = pl.pallas_call(
        functools.partial(joint_kernel, (owners, shards, cap, rows, kept, reduce_here)),
        out_shape=outputs,
        in_specs=[hbm] * len(arrays),
        out_specs=(hbm,) * 4,
        scratch_shapes=[
            exchange,
            exchange,
            exchange,
            exchange,
            pltpu.VMEM((shards, lab_part, width), bf16),
            pltpu.VMEM((outer, 2, shards // 2, 2, slot_rows, vocab), bf16),
            pltpu.VMEM((outer, 2, shards // 2, slot_rows, vocab), bf16),
            pltpu.VMEM((outer, 2, shards // 2, slot_rows, vocab), bf16),
            pltpu.VMEM((outer, 2, slot_rows, vocab), bf16),
            pltpu.VMEM((outer, 2, slot_rows, vocab), bf16),
            pltpu.VMEM((outer, 2, slot_rows, vocab), bf16),
            pltpu.VMEM((shards, lab_part, width), bf16),
            pltpu.VMEM((shards, lab_part, width), bf16),
            *fetched,
            pltpu.VMEM(w_out.shape, bf16),
            pltpu.VMEM(w_enc.shape[::-1], bf16),
            pltpu.VMEM(w_dec.shape[::-1], bf16),
            *(pltpu.VMEM(output.shape, output.dtype) for output in outputs),
            pltpu.SemaphoreType.DMA((2, 2, owners)),
            pltpu.SemaphoreType.DMA((2, 2, shards)),
            pltpu.SemaphoreType.DMA((2, outer, 2)),
            pltpu.SemaphoreType.DMA((2, outer, 2)),
            pltpu.SemaphoreType.DMA((len(arrays),)),
            pltpu.SemaphoreType.DMA((len(outputs),)),
        ],
        compiler_params=pltpu.CompilerParams(
            collective_id=0, has_side_effects=True, vmem_limit_bytes=VMEM_BYTES
        ),
    )(*arrays)
    tail = ()
    if not reduce_here:
        *results, grad_w = results
        tail = (lax.psum_scatter(grad_w, ("dp", "frame"), scatter_dimension=0, tiled=True),)
    logp, *others = pl.pallas_call(
        finish_kernel,
        out_shape=tuple(jax.ShapeDtypeStruct(array.shape, array.dtype) for array in results),
        in_specs=[hbm] * len(results),
        out_specs=(hbm,) * len(results),
        scratch_shapes=[
            *(pltpu.VMEM(array.shape, array.dtype) for array in results),
            pltpu.SemaphoreType.DMA((len(results),)),
            pltpu.SemaphoreType.DMA((len(results),)),
        ],
        compiler_params=pltpu.CompilerParams(vmem_limit_bytes=VMEM_BYTES),
    )(*results)
    return (logp.T, *others, *tail)


def solution(mesh):
    rows = P(("dp", "frame"), None)
    return jax.shard_map(
        shards_fn,
        mesh=mesh,
        in_specs=(
            rows,
            P(None, "frame", None),
            rows,
            P("dp", None),
            P(("dp", "frame")),
            P(("dp", "frame")),
            P(),
            P(),
            P(),
            P(),
            rows,
            rows,
        ),
        out_specs=(rows, rows, rows, rows),
        check_vma=False,
    )
```
